128 devices in a mesh: pool: 16 (over x_lo, z, core), head: 8 (over y, x_hi).
Axes of the slice: x: 4 (x_hi: 2, x_lo: 2; x = x_hi * 2 + x_lo), y: 4, z: 4, core: 2. Of those that a mesh axis runs over, the one named last changes fastest.
Arguments:
- hidden: bfloat16 [8192, 4096], P('pool')
- w_query: bfloat16 [4096, 4096], P(None, 'head'), may hold values from -0.09375 to 0.09375
- w_key: bfloat16 [4096, 4096], P(None, 'head'), may hold values from -0.09375 to 0.09375
- w_value: bfloat16 [4096, 4096], P(None, 'head'), may hold values from -0.09375 to 0.09375
- w_output: bfloat16 [4096, 4096], P('head'), may hold values from -6 to 6
- prefix_keys: bfloat16 [512, 16, 4096], P(('pool', 'head')), may hold values from -6 to 6
- prefix_values: bfloat16 [512, 16, 4096], P(('pool', 'head')), may hold values from -6 to 6
- block_slot: int32 [512], replicated, may hold values from 0 to 511, each once
- suffix_len: int32 [16], P('pool'), may hold values from 128 to 512, as said below
Outputs:
- mixed: bfloat16 [8192, 4096], P(('pool', 'head'))
The draws below stay inside these ranges and needn't reach their ends.
Inputs may be any that keep to these rules, and one draw needn't show every extreme that they name: `suffix_len`: one request has all 512 suffix tokens live.
All inputs are finite; a program needn't handle non-finite values.
Results may differ from the reference program's by a relative error of at most 0.04.
Values may be sent and summed in bfloat16 or wider, within the bound.
No kernel may reach another device: no remote copies, remote signals or barrier semaphores. Data moves between devices by JAX's collectives and lax.ppermute only.
A program may use at most 256 MiB of HBM per device.

```python
import math
import jax
import jax.numpy as jnp
from jax import lax

D = 4096
HQL = 4
HD = 128
BLOCK = 16
SUF = 512
HEADS = 32
NBLK = 512
PREFIX = 8192
TOKENS = 8192
N_POOL = 16
N_HEAD = 8


def draw_hidden(key, part):
    key = jax.random.fold_in(key, 11)
    first = jax.random.fold_in(key, 0)
    values = jax.random.normal(first, (TOKENS, D), jnp.float32)
    return values.astype(jnp.bfloat16)


def draw_suffix_len(key, part):
    key = jax.random.fold_in(key, 23)
    first, second = jax.random.split(key)
    lengths = jax.random.randint(first, (N_POOL,), SUF // 4, SUF + 1)
    chosen = jax.random.randint(second, (), 0, N_POOL)
    return jnp.where(jnp.arange(N_POOL) == chosen, SUF, lengths).astype(jnp.int32)


def block_scale(key, extent, cuts, low, high):
    factor_of, own = 1.0, jax.random.fold_in(key, 6)
    for dim, shards_of in cuts:
        heights = jnp.exp(jax.random.uniform(jax.random.fold_in(own, dim), (shards_of,), jnp.float32, low / len(cuts), high / len(cuts)))
        factor_of = factor_of * jnp.repeat(heights, extent[dim] // shards_of).reshape([-1 if axis == dim else 1 for axis in range(len(extent))])
    return factor_of


def centred(key, shape, scale, most, cuts=(), kind=jnp.bfloat16):
    gain = block_scale(key, shape, cuts, -0.22, 0.18) if cuts else 1.0
    array = jax.random.normal(key, shape, jnp.float32) * scale * gain
    return jnp.minimum(jnp.maximum(array, -most), most).astype(kind)


def setup_inputs(seed: int = 0) -> dict:
    seeds = jax.random.split(jax.random.key(seed), 10)
    hidden = draw_hidden(jax.random.fold_in(seeds[9], 71), 0)
    w_query = centred(seeds[1], (D, HEADS * HD), D ** -0.5, 0.09375, ((1, 8),))
    w_key = centred(seeds[2], (D, HEADS * HD), D ** -0.5, 0.09375, ((1, 8),))
    w_value = centred(seeds[3], (D, HEADS * HD), D ** -0.5, 0.09375, ((1, 8),))
    w_output = centred(seeds[4], (HEADS * HD, D), 1.0, 6.0, ((0, 8),))
    prefix_keys = centred(seeds[5], (NBLK, BLOCK, HEADS * HD), 1.0, 6.0, ((0, 128),))
    prefix_values = centred(seeds[6], (NBLK, BLOCK, HEADS * HD), 1.0, 6.0, ((0, 128),))
    block_slot = jax.random.permutation(seeds[7], NBLK).astype(jnp.int32)
    suffix_len = draw_suffix_len(jax.random.fold_in(seeds[9], 71), 0)
    return {"hidden": hidden, "w_query": w_query, "w_key": w_key, "w_value": w_value, "w_output": w_output, "prefix_keys": prefix_keys, "prefix_values": prefix_values, "block_slot": block_slot, "suffix_len": suffix_len}


def rope(values, positions):
    half = values.shape[-1] // 2
    freq = jnp.exp(-math.log(10000.0) * jnp.arange(half).astype(jnp.float32) * 2.0 / values.shape[-1])
    angle = positions.astype(jnp.float32)[:, None] * freq[None, :]
    cosine = jnp.cos(angle)[:, None, :]
    sine = jnp.sin(angle)[:, None, :]
    first = values[..., :half]
    second = values[..., half:]
    return jnp.concatenate([first * cosine - second * sine, first * sine + second * cosine], axis=-1)

def reference(hidden, w_query, w_key, w_value, w_output, prefix_keys, prefix_values, block_slot, suffix_len):
    heads = w_query.shape[1] // HD
    block_of_slot = jnp.zeros((NBLK,), jnp.int32).at[block_slot].set(jnp.arange(NBLK).astype(jnp.int32))
    prefix_pos = (block_of_slot[:, None] * BLOCK + jnp.arange(BLOCK).astype(jnp.int32)[None, :]).reshape(-1)
    key_prefix = rope(prefix_keys.astype(jnp.float32).reshape(PREFIX, heads, HD), prefix_pos).astype(jnp.bfloat16)
    value_prefix = prefix_values.reshape(PREFIX, heads, HD)
    scale = 1.0 / math.sqrt(HD)

    def request(items):
        rows, length = items
        spos = PREFIX + jnp.arange(SUF).astype(jnp.int32)
        query = rope(jnp.dot(rows, w_query, preferred_element_type=jnp.float32).reshape(SUF, heads, HD), spos).astype(jnp.bfloat16)
        key_suffix = rope(jnp.dot(rows, w_key, preferred_element_type=jnp.float32).reshape(SUF, heads, HD), spos).astype(jnp.bfloat16)
        value_suffix = jnp.dot(rows, w_value, preferred_element_type=jnp.float32).astype(jnp.bfloat16).reshape(SUF, heads, HD)
        keys = jnp.concatenate([key_prefix, key_suffix], axis=0)
        values = jnp.concatenate([value_prefix, value_suffix], axis=0)
        row_ids = jnp.arange(SUF)[:, None]
        col_ids = jnp.arange(SUF)[None, :]
        suffix_ok = (col_ids <= row_ids) & (col_ids < length)
        valid = jnp.concatenate([jnp.ones((SUF, PREFIX), bool), suffix_ok], axis=1)

        def one_head(parts):
            qh, kh, vh = parts
            scores = jnp.dot(qh, kh.T, preferred_element_type=jnp.float32) * scale
            scores = jnp.where(valid, scores, -jnp.inf)
            top = lax.optimization_barrier(jnp.max(scores, axis=1, keepdims=True))
            weights = jnp.exp(scores - top).astype(jnp.bfloat16)
            total = lax.optimization_barrier(jnp.sum(weights.astype(jnp.float32), axis=1, keepdims=True))
            return jnp.dot(weights, vh, preferred_element_type=jnp.float32) / total
        per_head = lax.map(one_head, (query.transpose(1, 0, 2), keys.transpose(1, 0, 2), values.transpose(1, 0, 2)))
        attended = per_head.transpose(1, 0, 2)
        attended = jnp.where(jnp.arange(SUF)[:, None, None] < length, attended, 0.0).astype(jnp.bfloat16)
        grouped = attended.reshape(SUF, N_HEAD, HQL * HD).astype(jnp.float32)
        weight_groups = w_output.reshape(N_HEAD, HQL * HD, D).astype(jnp.float32)
        partial_value = jnp.einsum('qsf,sfd->sqd', grouped, weight_groups).astype(jnp.bfloat16)
        partial_value = lax.optimization_barrier(partial_value)
        return lax.optimization_barrier(jnp.sum(partial_value.astype(jnp.float32), axis=0)).astype(jnp.bfloat16)
    outputs = lax.map(request, (hidden.reshape(N_POOL, SUF, D), suffix_len))
    return outputs.reshape(TOKENS, D)
```

```python
import functools
import math

import jax
import jax.numpy as jnp
import numpy as np
from jax import lax
from jax.experimental import pallas as pl
from jax.experimental.pallas import tpu as pltpu
from jax.sharding import Mesh, PartitionSpec as P

HD = 128
HQL = 4
BLOCK = 16
SUF = 512
PREFIX = 8192
WIDTH = HQL * HD
LOG2E = 1.4426950408889634
VMEM_LIMIT = 48 * 2**20
BF = jnp.bfloat16
F32 = jnp.float32


def frequencies():
    return np.exp(-math.log(10000.0) * np.arange(HD // 2) * 2.0 / HD)


def suffix_tables():
    angle = (PREFIX + np.arange(SUF))[:, None] * frequencies()[None, :]
    cosine, sine = np.cos(angle), np.sin(angle)
    return (
        np.concatenate([cosine, cosine], axis=1).astype(np.float32),
        np.concatenate([-sine, sine], axis=1).astype(np.float32),
    )


def call(kernel, name, flops, nbytes, **kwargs):
    return pl.pallas_call(
        kernel,
        name=name,
        cost_estimate=pl.CostEstimate(
            flops=int(flops), bytes_accessed=int(nbytes), transcendentals=0
        ),
        compiler_params=pltpu.CompilerParams(vmem_limit_bytes=VMEM_LIMIT),
        **kwargs,
    )


def turn(values, cosine, sine):
    return values * cosine + pltpu.roll(values, HD // 2, 1) * sine


def prep_kernel(place, slots, freq, keys, values, *outs):
    y, xhi, slot0 = place[0], place[1], place[2]
    shape = (slots.shape[0], slots.shape[1])
    block = (
        lax.broadcasted_iota(jnp.int32, shape, 0) * shape[1]
        + lax.broadcasted_iota(jnp.int32, shape, 1)
    ).astype(F32)
    rows = keys.shape[0]
    token = lax.broadcasted_iota(jnp.int32, (rows, HD), 0)
    position = jnp.zeros((rows, HD), F32)
    for i in range(rows // BLOCK):
        owner = jnp.sum(jnp.where(slots[...] == slot0 + i, block, 0.0))
        position = jnp.where(token // BLOCK == i, owner * BLOCK, position)
    position = position + (token % BLOCK).astype(F32)
    angle = position * freq[...]
    cosine = jnp.cos(angle)
    lane = lax.broadcasted_iota(jnp.int32, (rows, HD), 1)
    sine = jnp.sin(angle)
    sine = jnp.where(lane < HD // 2, -sine, sine)
    for d, out in enumerate(outs):
        target = lax.rem(y + d, 4)
        for part in range(2):
            group = 2 * target + (xhi if part == 0 else 1 - xhi)
            for h in range(HQL):
                at = pl.ds(pl.multiple_of(group * WIDTH + h * HD, HD), HD)
                to = pl.ds(h * HD, HD)
                turned = turn(keys[:, at].astype(F32), cosine, sine)
                out[pl.ds(part * 2 * rows, rows), to] = turned.astype(BF)
                out[pl.ds((part * 2 + 1) * rows, rows), to] = values[:, at]


def prepare(place, block_slot, keys, values):
    rows = keys.shape[0]
    freq = np.tile(frequencies(), 2)[None, :].astype(np.float32)
    vmem = pl.BlockSpec(memory_space=pltpu.VMEM)
    return call(
        prep_kernel,
        "prepare",
        1e7,
        3 * 2**20,
        in_specs=[pl.BlockSpec(memory_space=pltpu.SMEM)] + [vmem] * 4,
        out_specs=[vmem] * 4,
        out_shape=[jax.ShapeDtypeStruct((4 * rows, WIDTH), BF)] * 4,
    )(place, block_slot.reshape(4, -1), jnp.asarray(freq), keys, values)


def project_kernel(kinds, scale, hidden, *refs):
    n = len(kinds)
    weights, (cosine, sine) = refs[:n], refs[n : n + 2]
    outs, sums = refs[n + 2 : 2 * n + 2], refs[2 * n + 2 :]
    step = pl.program_id(0)
    for weight, total in zip(weights, sums):
        part = jnp.dot(hidden[...], weight[...], preferred_element_type=F32)

        @pl.when(step == 0)
        def _():
            total[...] = part

        @pl.when(step > 0)
        def _():
            total[...] += part

    @pl.when(step == pl.num_programs(0) - 1)
    def _():
        for kind, out, total in zip(kinds, outs, sums):
            for h in range(HQL):
                at = pl.ds(h * HD, HD)
                value = total[:, at]
                if kind != "v":
                    value = turn(value, cosine[...], sine[...])
                if kind == "q":
                    value = value * scale
                out[:, at] = value.astype(BF)


def project(kinds, hidden, weights, tables):
    rows, width = hidden.shape
    deep = 512
    n = len(kinds)
    whole = pl.BlockSpec((rows, HD), lambda i: (0, 0))
    return call(
        functools.partial(project_kernel, kinds, LOG2E / math.sqrt(HD)),
        "project_" + kinds,
        2 * n * rows * width * WIDTH,
        2 * (1 + n) * rows * width,
        grid=(width // deep,),
        in_specs=[pl.BlockSpec((rows, deep), lambda i: (0, i))]
        + [pl.BlockSpec((deep, WIDTH), lambda i: (i, 0))] * n
        + [whole] * 2,
        out_specs=[pl.BlockSpec((rows, WIDTH), lambda i: (0, 0))] * n,
        out_shape=[jax.ShapeDtypeStruct((rows, WIDTH), BF)] * n,
        scratch_shapes=[pltpu.VMEM((rows, WIDTH), F32)] * n,
    )(hidden, *weights, *tables)


def attend_tile(q, k, v_one, mask=None):
    s = lax.dot_general(q, k, (((1,), (1,)), ((), ())), preferred_element_type=F32)
    if mask is not None:
        s = jnp.where(mask, s, -1e30)
    top = jnp.max(s, axis=1, keepdims=True)
    p = jnp.exp2(s - top).astype(BF)
    both = jnp.dot(p, v_one, preferred_element_type=F32)
    return top, both[:, :HD], both[:, HD:]


def widen(v):
    return jnp.concatenate([v, jnp.ones_like(v)], axis=1)


def suffix_kernel(length, q_ref, k_ref, v_ref, o_ref, l_ref):
    h = pl.program_id(0)
    tile = 128
    for t in range(SUF // tile):
        rows, keys = pl.ds(t * tile, tile), (t + 1) * tile
        row = t * tile + lax.broadcasted_iota(jnp.int32, (tile, keys), 0)
        column = lax.broadcasted_iota(jnp.int32, (tile, keys), 1)
        mask = (column <= row) & (column < length[0])
        top, acc, total = attend_tile(
            q_ref[rows, :], k_ref[:keys, :], widen(v_ref[:keys, :]), mask
        )
        o_ref[rows, :] = acc / total
        lane = lax.broadcasted_iota(jnp.int32, (tile, HD), 1)
        l_ref[rows, :] = jnp.where(lane == h, top + jnp.log2(total), l_ref[rows, :])


def suffix_attention(length, q, k, v):
    head = pl.BlockSpec((SUF, HD), lambda h: (0, h))
    return call(
        suffix_kernel,
        "suffix_attention",
        4 * HQL * SUF * SUF * HD,
        4 * 2**20,
        grid=(HQL,),
        in_specs=[pl.BlockSpec(memory_space=pltpu.SMEM)] + [head] * 3,
        out_specs=[head, pl.BlockSpec((SUF, HD), lambda h: (0, 0))],
        out_shape=[
            jax.ShapeDtypeStruct((SUF, WIDTH), F32),
            jax.ShapeDtypeStruct((SUF, HD), F32),
        ],
    )(length, q, k, v)


def prefix_kernel(nq, nkv, held, last, *refs):
    qs, kvs = refs[:nq], refs[nq : nq + nkv]
    old, at = [], nq + nkv
    for has in held:
        old.append(refs[at : at + 2] if has else None)
        at += 2 * has
    outs, stats = refs[at : at + nq], refs[at + nq : at + 2 * nq]
    h = pl.program_id(0)
    half = kvs[0].shape[0] // 2
    k = jnp.concatenate([r[:half, :] for r in kvs], axis=0)
    v_one = widen(jnp.concatenate([r[half:, :] for r in kvs], axis=0))
    tile = 128
    lane = lax.broadcasted_iota(jnp.int32, (tile, HD), 1)
    for r in range(nq):
        for t in range(SUF // tile):
            rows = pl.ds(t * tile, tile)
            top, acc, total = attend_tile(qs[r][rows, :], k, v_one)
            if old[r] is not None:
                before = jnp.max(
                    jnp.where(lane == h, old[r][1][rows, :], -jnp.inf),
                    axis=1,
                    keepdims=True,
                )
                both = jnp.maximum(top, before)
                shrink, grow = jnp.exp2(before - both), jnp.exp2(top - both)
                total = shrink + grow * total
                acc = shrink * old[r][0][rows, :] + grow * acc
                top = both
            outs[r][rows, :] = (acc / total).astype(outs[r].dtype)
            keep = refs[-1].at[r] if last else stats[r]
            keep[rows, :] = jnp.where(lane == h, top + jnp.log2(total), keep[rows, :])
    if last:

        @pl.when(h == HQL - 1)
        def _():
            for r in range(nq):
                stats[r][...] = refs[-1][r].T[: stats[r].shape[0], :]


def prefix_attention(name, qs, kvs, states, last):
    nq, nkv = len(qs), len(kvs)
    held = [state is not None for state in states]
    head = pl.BlockSpec((SUF, HD), lambda h: (0, h))
    piece = pl.BlockSpec((kvs[0].shape[0], HD), lambda h: (0, h))
    stat = pl.BlockSpec((SUF, HD), lambda h: (0, 0))
    flat = pl.BlockSpec((8, SUF), lambda h: (0, 0))
    extra = [x for state in states if state is not None for x in state]
    tokens = nkv * kvs[0].shape[0] // 2
    out = call(
        functools.partial(prefix_kernel, nq, nkv, held, last),
        name,
        2 * 4 * nq * HQL * SUF * tokens * HD,
        nq * 4 * 2**20,
        grid=(HQL,),
        in_specs=[head] * nq + [piece] * nkv + [head, stat] * sum(held),
        out_specs=[head] * nq + [flat if last else stat] * nq,
        out_shape=[jax.ShapeDtypeStruct((SUF, WIDTH), BF if last else F32)] * nq
        + [jax.ShapeDtypeStruct((8, SUF) if last else (SUF, HD), F32)] * nq,
        scratch_shapes=[pltpu.VMEM((nq, SUF, HD), F32)] if last else [],
    )(*qs, *kvs, *extra)
    return list(zip(out[:nq], out[nq:]))


def output_kernel(n, length, *refs):
    parts, stats, weight, out, attended = refs[:n], refs[n : 2 * n], *refs[2 * n :]

    @pl.when(pl.program_id(0) == 0)
    def _():
        columns = []
        for stat in stats:
            tall = jnp.concatenate(
                [stat[...], jnp.zeros((HD - stat.shape[0], SUF), F32)], axis=0
            )
            columns.append(tall.T)
        top = functools.reduce(jnp.maximum, columns)
        shares = [jnp.exp2(c - top) for c in columns]
        total = functools.reduce(lambda a, b: a + b, shares)
        row = lax.broadcasted_iota(jnp.int32, (SUF, HD), 0)
        live = row < length[0]
        for h in range(HQL):
            at = pl.ds(h * HD, HD)
            acc = jnp.zeros((SUF, HD), F32)
            for share, part in zip(shares, parts):
                acc += (share / total)[:, h : h + 1] * part[:, at].astype(F32)
            attended[:, at] = jnp.where(live, acc, 0.0).astype(BF)

    out[...] = jnp.dot(
        attended[...], weight[...], preferred_element_type=F32
    ).astype(BF)


def output_projection(length, pieces, weight):
    n = len(pieces)
    width = weight.shape[1]
    wide = 1024
    whole = pl.BlockSpec((SUF, WIDTH), lambda i: (0, 0))
    flat = pl.BlockSpec((8, SUF), lambda i: (0, 0))
    return call(
        functools.partial(output_kernel, n),
        "output_projection",
        2 * SUF * WIDTH * width,
        12 * 2**20,
        grid=(width // wide,),
        in_specs=[pl.BlockSpec(memory_space=pltpu.SMEM)]
        + [whole] * n
        + [flat] * n
        + [pl.BlockSpec((WIDTH, wide), lambda i: (0, i))],
        out_specs=pl.BlockSpec((SUF, wide), lambda i: (0, i)),
        out_shape=jax.ShapeDtypeStruct((SUF, width), BF),
        scratch_shapes=[pltpu.VMEM((SUF, WIDTH), BF)],
    )(length, *[p[0] for p in pieces], *[p[1] for p in pieces], weight)


def shift(n, by):
    return [(i, (i + by) % n) for i in range(n)]


def body(
    hidden, w_query, w_key, w_value, w_output, prefix_keys, prefix_values, block_slot, suffix_len
):
    slots, block, feats = prefix_keys.shape
    device = lax.axis_index(("xlo", "z", "core", "y", "xhi"))
    y, xhi = lax.axis_index("y"), lax.axis_index("xhi")
    place = jnp.stack([y, xhi, device * slots]).astype(jnp.int32)
    tables = [jnp.asarray(t) for t in suffix_tables()]

    sent = prepare(
        place,
        block_slot,
        prefix_keys.reshape(slots * block, feats),
        prefix_values.reshape(slots * block, feats),
    )
    (q,) = project("q", hidden, [w_query], tables)
    got = [sent[0]] + [lax.ppermute(sent[d], "y", shift(4, d)) for d in (1, 2, 3)]
    qs = [q] + [lax.ppermute(q, "z", shift(4, d)) for d in (1, 2, 3)]
    k_suffix, v_suffix = project("kv", hidden, [w_key, w_value], tables)

    rows = slots * block

    def pack(first):
        return jnp.concatenate(
            [g[first : first + rows] for g in got]
            + [g[first + rows : first + 2 * rows] for g in got],
            axis=0,
        )

    near, far = pack(0), pack(2 * rows)
    cross = [(0, 3), (3, 0), (1, 2), (2, 1)]

    def core(x):
        return lax.ppermute(x, "core", shift(2, 1))

    near_x = lax.ppermute(near, "xlo", shift(2, 1))
    far_x = lax.ppermute(far, ("xlo", "xhi"), cross)
    far_xx = lax.ppermute(far_x, "xlo", shift(2, 1))

    own = suffix_attention(suffix_len, q, k_suffix, v_suffix)
    states = [own, None, None, None]
    states = prefix_attention("attend_near", qs, [near, core(near)], states, False)
    states = prefix_attention(
        "attend_middle", qs, [near_x, far_x, core(near_x), core(far_x)], states, False
    )
    final = [far_xx, core(far_xx)]
    pieces = []
    for d in (2, 1, 3, 0):
        part, stat = prefix_attention("attend_last", [qs[d]], final, [states[d]], True)[0]
        if d:
            part = lax.ppermute(part, "z", shift(4, -d))
            stat = lax.ppermute(stat, "z", shift(4, -d))
        pieces.append((part, stat))
    partial = output_projection(suffix_len, pieces, w_output)
    shares = lax.all_to_all(
        partial.reshape(8, SUF // 8, feats), ("y", "xhi"), split_axis=0, concat_axis=0
    )
    return jnp.sum(shares.astype(F32), axis=0).astype(BF)


def solution(mesh):
    fine = Mesh(
        mesh.devices.reshape(2, 4, 2, 4, 2), ("xlo", "z", "core", "y", "xhi")
    )
    pool, head = ("xlo", "z", "core"), ("y", "xhi")
    placed = (
        P(pool, None),
        P(None, head),
        P(None, head),
        P(None, head),
        P(head, None),
        P(pool + head, None, None),
        P(pool + head, None, None),
        P(),
        P(pool),
    )
    return jax.shard_map(
        body, mesh=fine, in_specs=placed, out_specs=P(pool + head, None), check_vma=False
    )
```

```python
import functools
import math

import jax
import jax.numpy as jnp
import numpy as np
from jax import lax
from jax.experimental import pallas as pl
from jax.experimental.pallas import tpu as pltpu
from jax.sharding import Mesh, PartitionSpec as P

HD = 128
HQL = 4
BLOCK = 16
SUF = 512
PREFIX = 8192
WIDTH = HQL * HD
LOG2E = 1.4426950408889634
EXTRA = 16
SLABS = 8
BF = jnp.bfloat16
F32 = jnp.float32


def frequencies():
    return np.exp(-math.log(10000.0) * np.arange(HD // 2) * 2.0 / HD)


def suffix_tables():
    angle = (PREFIX + np.arange(SUF))[:, None] * frequencies()[None, :]
    cosine, sine = np.cos(angle), np.sin(angle)
    return (
        np.concatenate([cosine, cosine], axis=1).astype(np.float32),
        np.concatenate([-sine, sine], axis=1).astype(np.float32),
    )


def call(kernel, name, vmem=24, flops=1, **kwargs):
    return pl.pallas_call(
        kernel,
        name=name,
        cost_estimate=pl.CostEstimate(flops=flops, bytes_accessed=1, transcendentals=0),
        compiler_params=pltpu.CompilerParams(vmem_limit_bytes=vmem * 2**20),
        **kwargs,
    )


def turn(values, cosine, sine):
    return values * cosine + pltpu.roll(values, HD // 2, 1) * sine


def prep_kernel(slots, freq, keys_hbm, values_hbm, *refs):
    outs, (keys, values, sems) = refs[:-3], refs[-3:]
    copies = [
        pltpu.make_async_copy(keys_hbm, keys, sems.at[0]),
        pltpu.make_async_copy(values_hbm, values, sems.at[1]),
    ]
    for copy in copies:
        copy.start()
    y, xhi = lax.axis_index("y"), lax.axis_index("xhi")
    chip = lax.axis_index("xlo") * 4 + lax.axis_index("z")
    device = (chip * 2 + lax.axis_index("core")) * 8 + y * 2 + xhi
    slot0 = device * (keys.shape[0] // BLOCK)
    shape = (slots.shape[0], slots.shape[1])
    block = (
        lax.broadcasted_iota(jnp.int32, shape, 0) * shape[1]
        + lax.broadcasted_iota(jnp.int32, shape, 1)
    ).astype(F32)
    rows = keys.shape[0]
    token = lax.broadcasted_iota(jnp.int32, (rows, HD), 0)
    position = jnp.zeros((rows, HD), F32)
    for i in range(rows // BLOCK):
        owner = jnp.sum(jnp.where(slots[...] == slot0 + i, block, 0.0))
        position = jnp.where(token // BLOCK == i, owner * BLOCK, position)
    position = position + (token % BLOCK).astype(F32)
    angle = position * freq[...]
    cosine = jnp.cos(angle)
    lane = lax.broadcasted_iota(jnp.int32, (rows, HD), 1)
    sine = jnp.sin(angle)
    sine = jnp.where(lane < HD // 2, -sine, sine)
    for kind, copy in enumerate(copies):
        copy.wait()
        for d, out in enumerate(outs):
            target = lax.rem(y + d, 4)
            for part in range(2):
                group = 2 * target + (xhi if part == 0 else 1 - xhi)
                to = pl.ds((part * 2 + kind) * rows, rows)
                for h in range(HQL):
                    at = pl.ds(pl.multiple_of(group * WIDTH + h * HD, HD), HD)
                    if kind == 0:
                        value = turn(keys[:, at].astype(F32), cosine, sine).astype(BF)
                    else:
                        value = values[:, at]
                    out[to, pl.ds(h * HD, HD)] = value


def prepare(block_slot, keys, values):
    rows = keys.shape[0]
    freq = np.tile(frequencies(), 2)[None, :].astype(np.float32)
    vmem = pl.BlockSpec(memory_space=pltpu.VMEM)
    return call(
        prep_kernel,
        "prepare",
        60,
        in_specs=[vmem] * 2
        + [pl.BlockSpec(memory_space=pltpu.HBM)] * 2,
        out_specs=[vmem] * 4,
        out_shape=[jax.ShapeDtypeStruct((4 * rows, WIDTH), BF)] * 4,
        scratch_shapes=[
            pltpu.VMEM(keys.shape, BF),
            pltpu.VMEM(values.shape, BF),
            pltpu.SemaphoreType.DMA((2,)),
        ],
    )(block_slot.reshape(4, -1), jnp.asarray(freq), keys, values)


def project_kernel(kinds, scale, fetched, hidden, cosine, sine, *refs):
    n = len(kinds)
    weights, outs, refs = refs[:n], refs[n : 2 * n], refs[2 * n :]
    rows = hidden
    if not fetched:
        rows, refs = refs[0], refs[1:]
    slabs, sems = refs[:n], refs[n]
    depth = hidden.shape[1]
    deep = depth // SLABS
    copies = []
    for i in range(SLABS):
        at = pl.ds(i * deep, deep)
        slab = [(w.at[at, :], v.at[at, :]) for w, v in zip(weights, slabs)]
        if not fetched:
            slab.append((hidden.at[:, at], rows.at[:, at]))
        copies.append(
            [
                pltpu.make_async_copy(src, dst, sems.at[i, j])
                for j, (src, dst) in enumerate(slab)
            ]
        )
        for copy in copies[-1]:
            copy.start()
    totals = [0.0] * n
    for i in range(SLABS):
        for copy in copies[i]:
            copy.wait()
        at = slice(i * deep, (i + 1) * deep)
        for j, slab in enumerate(slabs):
            totals[j] += jnp.dot(rows[:, at], slab[at, :], preferred_element_type=F32)
    for kind, out, total in zip(kinds, outs, totals):
        for h in range(HQL):
            at = slice(h * HD, (h + 1) * HD)
            value = total[:, at]
            if kind != "v":
                value = turn(value, cosine[...], sine[...])
            if kind == "q":
                value = value * scale
            out[:, at] = value.astype(BF)


def project(kinds, hidden, weights, tables, fetched):
    rows, depth = hidden.shape
    n = len(kinds)
    vmem = pl.BlockSpec(memory_space=pltpu.VMEM)
    hbm = pl.BlockSpec(memory_space=pltpu.HBM)
    more = not fetched
    return call(
        functools.partial(project_kernel, kinds, LOG2E / math.sqrt(HD), fetched),
        "project_" + kinds,
        40 if fetched else 50,
        in_specs=[vmem if fetched else hbm] + [vmem] * 2 + [hbm] * n,
        out_specs=[vmem] * (n + more),
        out_shape=[jax.ShapeDtypeStruct((rows, WIDTH), BF)] * n
        + [jax.ShapeDtypeStruct((rows, depth), BF)] * more,
        scratch_shapes=[pltpu.VMEM((depth, WIDTH), BF)] * n
        + [pltpu.SemaphoreType.DMA((SLABS, n + more))],
    )(hidden, *tables, *weights)


def pack_kernel(n, *refs):
    got, outs = refs[:n], refs[n:]
    rows = got[0].shape[0] // 4
    for part, out in enumerate(outs):
        for kind in range(2):
            for i, piece in enumerate(got):
                at = pl.ds((kind * n + i) * rows, rows)
                out[at, :] = piece[pl.ds((2 * part + kind) * rows, rows), :]


def pack(got):
    rows, width = got[0].shape
    vmem = pl.BlockSpec(memory_space=pltpu.VMEM)
    return call(
        functools.partial(pack_kernel, len(got)),
        "pack",
        in_specs=[vmem] * len(got),
        out_specs=[vmem] * 2,
        out_shape=[jax.ShapeDtypeStruct((len(got) * rows // 2, width), BF)] * 2,
    )(*got)


def widen(v):
    return jnp.concatenate([v, jnp.ones_like(v)], axis=1)


def suffix_kernel(length, q_ref, k_ref, v_ref, sum_ref, top_ref):
    tile = 128
    for t in range(SUF // tile):
        rows, keys = pl.ds(t * tile, tile), (t + 1) * tile
        row = t * tile + lax.broadcasted_iota(jnp.int32, (tile, keys), 0)
        column = lax.broadcasted_iota(jnp.int32, (tile, keys), 1)
        mask = (column <= row) & (column < length[0])
        for h in range(HQL):
            head = slice(h * HD, (h + 1) * HD)
            s = lax.dot_general(
                q_ref[rows, head],
                k_ref[:keys, head],
                (((1,), (1,)), ((), ())),
                preferred_element_type=F32,
            )
            s = jnp.where(mask, s, -1e30)
            top = jnp.max(s, axis=1, keepdims=True)
            p = jnp.exp2(s - top).astype(BF)
            sum_ref[rows, 2 * h * HD : 2 * (h + 1) * HD] = jnp.dot(
                p, widen(v_ref[:keys, head]), preferred_element_type=F32
            )
            top_ref[rows, head] = jnp.broadcast_to(top, (tile, HD))


def suffix_attention(length, q, k, v):
    vmem = pl.BlockSpec(memory_space=pltpu.VMEM)
    return call(
        suffix_kernel,
        "suffix_attention",
        flops=2 * 10**10,
        in_specs=[pl.BlockSpec(memory_space=pltpu.SMEM)] + [vmem] * 3,
        out_specs=[vmem] * 2,
        out_shape=STATE,
    )(length, q, k, v)


def split_log(log):
    high = log.astype(BF)
    rest = log - high.astype(F32)
    middle = rest.astype(BF)
    return high, middle, (rest - middle.astype(F32)).astype(BF)


def prefix_kernel(nq, nkv, used, held, last, *refs):
    qs, kvs = refs[:nq], refs[nq : nq + nkv]
    old, at = [], nq + nkv
    for has in held:
        old.append(refs[at : at + 2] if has else None)
        at += 2 * has
    outs = refs[at:]
    half = kvs[0].shape[0] // 2
    tile = 256

    def one_tile(h, r, rows):
        head = slice(h * HD, (h + 1) * HD)
        wide = slice(2 * h * HD, 2 * (h + 1) * HD)
        n = used[r]
        k = jnp.concatenate([kv[:half, head] for kv in kvs[:n]], axis=0)
        v = jnp.concatenate([kv[half:, head] for kv in kvs[:n]], axis=0)
        s = lax.dot_general(
            qs[r][rows, head],
            k,
            (((1,), (1,)), ((), ())),
            preferred_element_type=F32,
        )
        top = jnp.broadcast_to(jnp.max(s, axis=1, keepdims=True), (tile, HD))
        if old[r] is not None:
            before = old[r][1][rows, head]
            top = jnp.maximum(before, top)
        p = jnp.exp2(s - jnp.concatenate([top] * (n * half // HD), axis=1)).astype(BF)
        both = jnp.dot(p, widen(v), preferred_element_type=F32)
        if old[r] is not None:
            shrink = jnp.exp2(before - top)
            both += jnp.concatenate([shrink] * 2, axis=1) * old[r][0][rows, wide]
        if not last:
            outs[2 * r][rows, wide] = both
            outs[2 * r + 1][rows, head] = top
            return []
        acc, total = both[:, :HD], both[:, HD:]
        outs[r][rows, head] = (acc / total).astype(BF)
        log = top + jnp.log2(total)
        return [log[i : i + HD].T[:1] for i in range(0, tile, HD)]

    if not last:

        @pl.loop(0, SUF // tile)
        def _(t):
            rows = pl.ds(pl.multiple_of(t * tile, tile), tile)
            for h in range(HQL):
                for r in range(nq):
                    one_tile(h, r, rows)

        return
    for h in range(HQL):
        for r in range(nq):
            logs = []
            for t in range(SUF // tile):
                logs += one_tile(h, r, pl.ds(t * tile, tile))
            rest = jnp.zeros((EXTRA - 3 * len(logs), HD), BF)
            parts = split_log(jnp.concatenate(logs, axis=0))
            tail = jnp.concatenate([*parts, rest], axis=0)
            outs[r][SUF:, h * HD : (h + 1) * HD] = tail


STATE = [
    jax.ShapeDtypeStruct((SUF, 2 * WIDTH), F32),
    jax.ShapeDtypeStruct((SUF, WIDTH), F32),
]


def prefix_attention(name, qs, kvs, used, states, last):
    nq, nkv = len(qs), len(kvs)
    held = [state is not None for state in states]
    extra = [x for state in states if state is not None for x in state]
    vmem = pl.BlockSpec(memory_space=pltpu.VMEM)
    message = [jax.ShapeDtypeStruct((SUF + EXTRA, WIDTH), BF)]
    out = call(
        functools.partial(prefix_kernel, nq, nkv, used, held, last),
        name,
        in_specs=[vmem] * (nq + nkv + len(extra)),
        out_specs=[vmem] * (nq if last else 2 * nq),
        out_shape=(message if last else STATE) * nq,
    )(*qs, *kvs, *extra)
    return list(out) if last else [out[i : i + 2] for i in range(0, 2 * nq, 2)]


def combine(parts, length, attended):
    tile = HD
    count = SUF // tile
    row = lax.broadcasted_iota(jnp.int32, (tile, HD), 0)
    for h in range(HQL):
        at = pl.ds(h * HD, HD)
        logs = []
        for part in parts:
            tail = part[SUF:, at].astype(F32)
            logs.append(
                tail[:count] + tail[count : 2 * count] + tail[2 * count : 3 * count]
            )
        top = functools.reduce(jnp.maximum, logs)
        shares = [jnp.exp2(log - top) for log in logs]
        total = functools.reduce(lambda a, b: a + b, shares)
        shares = [share / total for share in shares]
        for t in range(count):
            rows = pl.ds(t * tile, tile)
            acc = jnp.zeros((tile, HD), F32)
            for share, part in zip(shares, parts):
                wide = jnp.broadcast_to(share[t : t + 1, :], (tile, HD)).T
                acc += wide * part[rows, at].astype(F32)
            live = t * tile + row < length[0]
            attended[rows, at] = jnp.where(live, acc, 0.0).astype(BF)


def product(rows, weight, out):
    out[...] = jnp.dot(rows[...], weight[...], preferred_element_type=F32).astype(BF)


def first_half_kernel(n, length, *refs):
    parts, (weight, theirs, ours, by_y, attended, by_x) = refs[:n], refs[n:]
    y, xhi = lax.axis_index("y"), lax.axis_index("xhi")
    few = SUF // 8

    @pl.when(pl.program_id(0) == 0)
    def _():
        combine(parts, length, attended)
        for d in range(4):
            target = lax.rem(y + d, 4)
            at = pl.ds(pl.multiple_of(target * 2 * few, 2 * few), 2 * few)
            by_y[pl.ds(d * 2 * few, 2 * few), :] = attended[at, :]
            for part in range(2):
                group = 2 * d + (1 - xhi if part == 0 else xhi)
                at = pl.ds(pl.multiple_of(group * few, few), few)
                by_x[pl.ds((part * 4 + d) * few, few), :] = attended[at, :]

    half = SUF // 2
    product(by_x.at[pl.ds(0, half)], weight, theirs)
    product(by_x.at[pl.ds(half, half)], weight, ours)


def first_half(length, parts, weight):
    n = len(parts)
    width = weight.shape[1] // 2
    wide = 1024
    half = SUF // 2
    whole = pl.BlockSpec((SUF + EXTRA, WIDTH), lambda i: (0, 0))
    return call(
        functools.partial(first_half_kernel, n),
        "first_half",
        grid=(width // wide,),
        in_specs=[pl.BlockSpec(memory_space=pltpu.SMEM)]
        + [whole] * n
        + [pl.BlockSpec((WIDTH, wide), lambda i: (0, i))],
        out_specs=[pl.BlockSpec((half, wide), lambda i: (0, i))] * 2
        + [pl.BlockSpec((SUF, WIDTH), lambda i: (0, 0))],
        out_shape=[jax.ShapeDtypeStruct((half, width), BF)] * 2
        + [jax.ShapeDtypeStruct((SUF, WIDTH), BF)],
        scratch_shapes=[pltpu.VMEM((SUF, WIDTH), BF)] * 2,
    )(length, *parts, weight)


def second_half_kernel(by_y, weight, *outs):
    rows = outs[0].shape[0]
    for d, out in enumerate(outs):
        product(by_y.at[pl.ds(d * rows, rows)], weight, out)


def second_half(by_y, weight):
    width = weight.shape[1] // 2
    wide = 1024
    skip = width // wide
    return call(
        second_half_kernel,
        "second_half",
        grid=(width // wide,),
        in_specs=[
            pl.BlockSpec((SUF, WIDTH), lambda i: (0, 0)),
            pl.BlockSpec((WIDTH, wide), lambda i: (0, i + skip)),
        ],
        out_specs=[pl.BlockSpec((SUF // 4, wide), lambda i: (0, i))] * 4,
        out_shape=[jax.ShapeDtypeStruct((SUF // 4, width), BF)] * 4,
    )(by_y, weight)


def sum_x_kernel(ours, theirs, *outs):
    y = lax.axis_index("y")
    rows = outs[0].shape[0]
    for d, out in enumerate(outs):
        at = pl.ds(pl.multiple_of(lax.rem(y + d, 4) * rows, rows), rows)
        out[...] = (ours[at, :].astype(F32) + theirs[at, :].astype(F32)).astype(BF)


def sum_x(ours, theirs):
    rows, width = ours.shape
    wide = 512
    return call(
        sum_x_kernel,
        "sum_x",
        grid=(width // wide,),
        in_specs=[pl.BlockSpec((rows, wide), lambda i: (0, i))] * 2,
        out_specs=[pl.BlockSpec((rows // 4, wide), lambda i: (0, i))] * 4,
        out_shape=[jax.ShapeDtypeStruct((rows // 4, width), BF)] * 4,
    )(ours, theirs)


def add_up(refs, at=slice(None)):
    return functools.reduce(lambda a, b: a + b, [r[at, :].astype(F32) for r in refs])


def sum_y_kernel(n, *refs):
    parts, (theirs, ours) = refs[:n], refs[n:]
    xhi = lax.axis_index("xhi")
    rows = ours.shape[0]
    for part, out in ((1 - xhi, theirs), (xhi, ours)):
        at = pl.ds(pl.multiple_of(part * rows, rows), rows)
        out[...] = add_up(parts, at).astype(BF)


def sum_y(parts):
    rows, width = parts[0].shape
    wide = 512
    return call(
        functools.partial(sum_y_kernel, len(parts)),
        "sum_y",
        grid=(width // wide,),
        in_specs=[pl.BlockSpec((rows, wide), lambda i: (0, i))] * len(parts),
        out_specs=[pl.BlockSpec((rows // 2, wide), lambda i: (0, i))] * 2,
        out_shape=[jax.ShapeDtypeStruct((rows // 2, width), BF)] * 2,
    )(*parts)


def finish_kernel(n, *refs):
    left, right, out = refs[:n], refs[n:-1], refs[-1]
    width = left[0].shape[1]
    out[:, :width] = add_up(left).astype(BF)
    out[:, width:] = add_up(right).astype(BF)


def finish(left, right):
    rows, width = left[0].shape
    vmem = pl.BlockSpec(memory_space=pltpu.VMEM)
    return call(
        functools.partial(finish_kernel, len(left)),
        "finish",
        in_specs=[vmem] * (len(left) + len(right)),
        out_specs=vmem,
        out_shape=jax.ShapeDtypeStruct((rows, 2 * width), BF),
    )(*left, *right)


def shift(n, by):
    return [(i, (i + by) % n) for i in range(n)]


def in_order(values, *others):
    return lax.optimization_barrier((*values, *others))[: len(values)]


def body(
    hidden, w_query, w_key, w_value, w_output, prefix_keys, prefix_values, block_slot, suffix_len
):
    slots, block, feats = prefix_keys.shape
    rows = slots * block
    tables = [jnp.asarray(t) for t in suffix_tables()]

    def core(x):
        return lax.ppermute(x, "core", shift(2, 1))

    def along_z(x, by):
        return lax.ppermute(x, "z", shift(4, by))

    sent = prepare(
        block_slot, prefix_keys.reshape(rows, feats), prefix_values.reshape(rows, feats)
    )
    got = [sent[0]] + [lax.ppermute(sent[d], "y", shift(4, d)) for d in (1, 2, 3)]

    (hidden,) = in_order([hidden], sent[0])
    q, hidden = project("q", hidden, [w_query], tables, False)
    q1, q3 = along_z(q, 1), along_z(q, -1)
    k_suffix, v_suffix = project("kv", hidden, [w_key, w_value], tables, True)

    got = in_order(got, k_suffix)
    near, far = pack(got)
    near_x = lax.ppermute(near, "xlo", shift(2, 1))
    far_x = lax.ppermute(far, ("xlo", "xhi"), [(0, 3), (3, 0), (1, 2), (2, 1)])
    q2 = along_z(in_order([q], near)[0], 2)
    (k_suffix,) = in_order([k_suffix], near)
    own = suffix_attention(suffix_len, q, k_suffix, v_suffix)

    q1, q3 = in_order([q1, q3], own[0])
    near_c = core(in_order([near], q1, q3)[0])
    state0, state1, state3 = prefix_attention(
        "attend_near", [q, q1, q3], [near, near_c], [2, 2, 2], [own, None, None], False
    )
    near_x, far_x = in_order([near_x, far_x], state0[0])
    far_xx = lax.ppermute(far_x, "xlo", shift(2, 1))
    states = prefix_attention(
        "attend_middle",
        [q, q1, q3, q2],
        [near_x, far_x, core(near_x), core(far_x), near, near_c],
        [4, 4, 4, 6],
        [state0, state1, state3, None],
        False,
    )
    (far_xx,) = in_order([far_xx], states[0][0])
    final = [far_xx, core(far_xx)]
    parts = []
    for state, query, back in zip(
        [states[3], states[1], states[2], states[0]], [q2, q1, q3, q], [2, -1, 1, 0]
    ):
        (part,) = prefix_attention("attend_last", [query], final, [2], [state], True)
        parts.append(along_z(part, back) if back else part)
    parts[:3] = in_order(parts[:3], parts[3])
    theirs, ours, by_y = first_half(suffix_len, parts, w_output)
    theirs = lax.ppermute(theirs, "xhi", shift(2, 1))
    cut = second_half(by_y, w_output)
    cut = [cut[0]] + [lax.ppermute(cut[d], "y", shift(4, d)) for d in (1, 2, 3)]
    left = sum_x(ours, theirs)
    left = [left[0]] + [lax.ppermute(left[d], "y", shift(4, d)) for d in (1, 2, 3)]
    theirs, ours = sum_y(cut)
    return finish(left, [ours, lax.ppermute(theirs, "xhi", shift(2, 1))])


def solution(mesh):
    fine = Mesh(
        mesh.devices.reshape(2, 4, 2, 4, 2), ("xlo", "z", "core", "y", "xhi")
    )
    pool, head = ("xlo", "z", "core"), ("y", "xhi")
    placed = (
        P(pool, None),
        P(None, head),
        P(None, head),
        P(None, head),
        P(head, None),
        P(pool + head, None, None),
        P(pool + head, None, None),
        P(),
        P(pool),
    )
    return jax.shard_map(
        body, mesh=fine, in_specs=placed, out_specs=P(pool + head, None), check_vma=False
    )
```

```python
import functools
import math

import jax
import jax.numpy as jnp
import numpy as np
from jax import lax
from jax.experimental import pallas as pl
from jax.experimental.pallas import tpu as pltpu
from jax.sharding import Mesh, PartitionSpec as P

HD = 128
HQL = 4
BLOCK = 16
SUF = 512
PREFIX = 8192
WIDTH = HQL * HD
LOG2E = 1.4426950408889634
EXTRA = 16
COST = 5 * 10**9
SUFFIX_COST = 1
NEAR_COST = 10**10
PACK_COST = 4 * 10**9
PIECE = 32
SLABS = 8
BF = jnp.bfloat16
F32 = jnp.float32


def frequencies():
    return np.exp(-math.log(10000.0) * np.arange(HD // 2) * 2.0 / HD)


def suffix_tables():
    angle = (PREFIX + np.arange(SUF))[:, None] * frequencies()[None, :]
    cosine, sine = np.cos(angle), np.sin(angle)
    return (
        np.concatenate([cosine, cosine], axis=1).astype(np.float32),
        np.concatenate([-sine, sine], axis=1).astype(np.float32),
    )


def pieces_of_rows():
    count = SUF // PIECE // 2
    return [
        ((half * count + device) * PIECE, (2 * device + half) * PIECE)
        for half in range(2)
        for device in range(count)
    ]


def place_of_row(row):
    half, inside = row // (SUF // 2), row % (SUF // 2)
    return (2 * (inside // PIECE) + half) * PIECE + inside % PIECE


def call(kernel, name, vmem=24, flops=1, **kwargs):
    return pl.pallas_call(
        kernel,
        name=name,
        cost_estimate=pl.CostEstimate(flops=flops, bytes_accessed=1, transcendentals=0),
        compiler_params=pltpu.CompilerParams(vmem_limit_bytes=vmem * 2**20),
        **kwargs,
    )


def turn(values, cosine, sine):
    return values * cosine + pltpu.roll(values, HD // 2, 1) * sine


def prep_kernel(slots, freq, keys_hbm, values_hbm, *refs):
    outs, (keys, values, sems) = refs[:-3], refs[-3:]
    copies = [
        pltpu.make_async_copy(keys_hbm, keys, sems.at[0]),
        pltpu.make_async_copy(values_hbm, values, sems.at[1]),
    ]
    for copy in copies:
        copy.start()
    y, xhi = lax.axis_index("y"), lax.axis_index("xhi")
    chip = lax.axis_index("xlo") * 4 + lax.axis_index("z")
    device = (chip * 2 + lax.axis_index("core")) * 8 + y * 2 + xhi
    slot0 = device * (keys.shape[0] // BLOCK)
    shape = (slots.shape[0], slots.shape[1])
    block = (
        lax.broadcasted_iota(jnp.int32, shape, 0) * shape[1]
        + lax.broadcasted_iota(jnp.int32, shape, 1)
    ).astype(F32)
    rows = keys.shape[0]
    token = lax.broadcasted_iota(jnp.int32, (rows, HD), 0)
    position = jnp.zeros((rows, HD), F32)
    for i in range(rows // BLOCK):
        owner = jnp.sum(jnp.where(slots[...] == slot0 + i, block, 0.0))
        position = jnp.where(token // BLOCK == i, owner * BLOCK, position)
    position = position + (token % BLOCK).astype(F32)
    angle = position * freq[...]
    cosine = jnp.cos(angle)
    lane = lax.broadcasted_iota(jnp.int32, (rows, HD), 1)
    sine = jnp.sin(angle)
    sine = jnp.where(lane < HD // 2, -sine, sine)
    for kind, copy in enumerate(copies):
        copy.wait()
        for d, out in enumerate(outs):
            target = lax.rem(y + d, 4)
            for part in range(2):
                group = 2 * target + (xhi if part == 0 else 1 - xhi)
                to = pl.ds((part * 2 + kind) * rows, rows)
                for h in range(HQL):
                    at = pl.ds(pl.multiple_of(group * WIDTH + h * HD, HD), HD)
                    if kind == 0:
                        value = turn(keys[:, at].astype(F32), cosine, sine).astype(BF)
                    else:
                        value = values[:, at]
                    out[to, pl.ds(h * HD, HD)] = value


def prepare(block_slot, keys, values):
    rows = keys.shape[0]
    freq = np.tile(frequencies(), 2)[None, :].astype(np.float32)
    vmem = pl.BlockSpec(memory_space=pltpu.VMEM)
    return call(
        prep_kernel,
        "prepare",
        60,
        in_specs=[vmem] * 2
        + [pl.BlockSpec(memory_space=pltpu.HBM)] * 2,
        out_specs=[vmem] * 4,
        out_shape=[jax.ShapeDtypeStruct((4 * rows, WIDTH), BF)] * 4,
        scratch_shapes=[
            pltpu.VMEM(keys.shape, BF),
            pltpu.VMEM(values.shape, BF),
            pltpu.SemaphoreType.DMA((2,)),
        ],
    )(block_slot.reshape(4, -1), jnp.asarray(freq), keys, values)


def project_kernel(kinds, scale, *refs):
    n = len(kinds)
    hidden, weights, tables, outs = refs[0], refs[1 : n + 1], refs[n + 1 : n + 3], refs[n + 3 :]
    outs, (rows, *slabs), turns, sems = outs[:n], outs[n : 2 * n + 1], outs[-3:-1], outs[-1]
    depth = hidden.shape[1]
    deep = depth // SLABS
    copies = []
    for i in range(SLABS):
        at = pl.ds(i * deep, deep)
        slab = [(hidden.at[:, at], rows.at[:, at])]
        slab += [(w.at[at, :], v.at[at, :]) for w, v in zip(weights, slabs)]
        copies.append(
            [
                pltpu.make_async_copy(src, dst, sems.at[i, j])
                for j, (src, dst) in enumerate(slab)
            ]
        )
    copies.append(
        [
            pltpu.make_async_copy(src, dst, sems.at[SLABS, j])
            for j, (src, dst) in enumerate(zip(tables, turns))
        ]
    )
    for group in copies:
        for copy in group:
            copy.start()
    totals = [0.0] * n
    for i in range(SLABS):
        for copy in copies[i]:
            copy.wait()
        at = slice(i * deep, (i + 1) * deep)
        for j, slab in enumerate(slabs):
            totals[j] += jnp.dot(rows[:, at], slab[at, :], preferred_element_type=F32)
    for copy in copies[SLABS]:
        copy.wait()
    cosine, sine = turns
    for kind, out, total in zip(kinds, outs, totals):
        for h in range(HQL):
            at = slice(h * HD, (h + 1) * HD)
            value = total[:, at]
            if kind != "v":
                value = turn(value, cosine[...], sine[...])
            if kind == "q":
                for to, origin in pieces_of_rows():
                    rows_to = pl.ds(to, PIECE)
                    out[rows_to, at] = (value[origin : origin + PIECE] * scale).astype(BF)
            else:
                out[:, at] = value.astype(BF)


def project(kinds, hidden, weights, tables):
    rows, depth = hidden.shape
    n = len(kinds)
    hbm = pl.BlockSpec(memory_space=pltpu.HBM)
    return call(
        functools.partial(project_kernel, kinds, LOG2E / math.sqrt(HD)),
        "project_" + kinds,
        60,
        1,
        in_specs=[hbm] * (n + 3),
        out_specs=[pl.BlockSpec(memory_space=pltpu.VMEM)] * n,
        out_shape=[jax.ShapeDtypeStruct((rows, WIDTH), BF)] * n,
        scratch_shapes=[pltpu.VMEM((rows, depth), BF)]
        + [pltpu.VMEM((depth, WIDTH), BF)] * n
        + [pltpu.VMEM((rows, HD), F32)] * 2
        + [pltpu.SemaphoreType.DMA((SLABS + 1, max(n + 1, 2)))],
    )(hidden, *weights, *tables)


def pack_kernel(n, *refs):
    got, outs = refs[:n], refs[n:]
    rows = got[0].shape[0] // 4
    for part, out in enumerate(outs):
        for kind in range(2):
            for i, piece in enumerate(got):
                at = pl.ds((kind * n + i) * rows, rows)
                out[at, :] = piece[pl.ds((2 * part + kind) * rows, rows), :]


def pack(got):
    rows, width = got[0].shape
    vmem = pl.BlockSpec(memory_space=pltpu.VMEM)
    return call(
        functools.partial(pack_kernel, len(got)),
        "pack",
        flops=PACK_COST,
        in_specs=[vmem] * len(got),
        out_specs=[vmem] * 2,
        out_shape=[jax.ShapeDtypeStruct((len(got) * rows // 2, width), BF)] * 2,
    )(*got)


def widen(v):
    return jnp.concatenate([v, jnp.ones_like(v)], axis=1)


def suffix_kernel(length, q_ref, k_ref, v_ref, sum_ref, top_ref):
    tile = 128
    for t in range(SUF // tile):
        rows, keys = pl.ds(t * tile, tile), (t % 2 + 1) * SUF // 2
        row = place_of_row(t * tile + lax.broadcasted_iota(jnp.int32, (tile, keys), 0))
        column = lax.broadcasted_iota(jnp.int32, (tile, keys), 1)
        mask = (column <= row) & (column < length[0])
        for h in range(HQL):
            head = slice(h * HD, (h + 1) * HD)
            s = lax.dot_general(
                q_ref[rows, head],
                k_ref[:keys, head],
                (((1,), (1,)), ((), ())),
                preferred_element_type=F32,
            )
            s = jnp.where(mask, s, -1e30)
            top = jnp.max(s, axis=1, keepdims=True)
            p = jnp.exp2(s - top).astype(BF)
            sum_ref[rows, 2 * h * HD : 2 * (h + 1) * HD] = jnp.dot(
                p, widen(v_ref[:keys, head]), preferred_element_type=F32
            )
            top_ref[rows, head] = jnp.broadcast_to(top, (tile, HD))


def suffix_attention(length, q, k, v):
    vmem = pl.BlockSpec(memory_space=pltpu.VMEM)
    return call(
        suffix_kernel,
        "suffix_attention",
        flops=SUFFIX_COST,
        in_specs=[pl.BlockSpec(memory_space=pltpu.SMEM)] + [vmem] * 3,
        out_specs=[vmem] * 2,
        out_shape=STATE,
    )(length, q, k, v)


def split_log(log):
    high = log.astype(BF)
    rest = log - high.astype(F32)
    middle = rest.astype(BF)
    return high, middle, (rest - middle.astype(F32)).astype(BF)


def prefix_kernel(nq, nkv, used, held, halves, *refs):
    qs, kvs = refs[:nq], refs[nq : nq + nkv]
    old, at = [], nq + nkv
    for has in held:
        old.append(refs[at : at + 2] if has else None)
        at += 2 * has
    outs = refs[at:]
    half = kvs[0].shape[0] // 2
    tile = SUF // 2

    def one_tile(h, r, rows, out=None):
        head = slice(h * HD, (h + 1) * HD)
        wide = slice(2 * h * HD, 2 * (h + 1) * HD)
        n = used[r]
        k = jnp.concatenate([kv[:half, head] for kv in kvs[:n]], axis=0)
        v = jnp.concatenate([kv[half:, head] for kv in kvs[:n]], axis=0)
        s = lax.dot_general(
            qs[r][rows, head],
            k,
            (((1,), (1,)), ((), ())),
            preferred_element_type=F32,
        )
        top = jnp.broadcast_to(jnp.max(s, axis=1, keepdims=True), (tile, HD))
        if old[r] is not None:
            before = old[r][1][rows, head]
            top = jnp.maximum(before, top)
        p = jnp.exp2(s - jnp.concatenate([top] * (n * half // HD), axis=1)).astype(BF)
        both = jnp.dot(p, widen(v), preferred_element_type=F32)
        if old[r] is not None:
            shrink = jnp.exp2(before - top)
            both += jnp.concatenate([shrink] * 2, axis=1) * old[r][0][rows, wide]
        if not halves:
            outs[2 * r][rows, wide] = both
            outs[2 * r + 1][rows, head] = top
            return
        acc, total = both[:, :HD], both[:, HD:]
        out[:tile, head] = (acc / total).astype(BF)
        log = top + jnp.log2(total)
        logs = [log[i : i + HD].T[:1] for i in range(0, tile, HD)]
        rest = jnp.zeros((EXTRA - 3 * len(logs), HD), BF)
        parts = split_log(jnp.concatenate(logs, axis=0))
        out[tile:, head] = jnp.concatenate([*parts, rest], axis=0)

    if not halves:

        @pl.loop(0, SUF // tile)
        def _(t):
            rows = pl.ds(pl.multiple_of(t * tile, tile), tile)
            for h in range(HQL):
                for r in range(nq):
                    one_tile(h, r, rows)

        return
    for h in range(HQL):
        for r in range(nq):
            for i, t in enumerate(halves):
                out = outs[r * len(halves) + i]
                one_tile(h, r, pl.ds(t * tile, tile), out)


STATE = [
    jax.ShapeDtypeStruct((SUF, 2 * WIDTH), F32),
    jax.ShapeDtypeStruct((SUF, WIDTH), F32),
]


def prefix_attention(name, qs, kvs, used, states, halves=(), cost=1):
    nq, nkv = len(qs), len(kvs)
    held = [state is not None for state in states]
    extra = [x for state in states if state is not None for x in state]
    vmem = pl.BlockSpec(memory_space=pltpu.VMEM)
    message = jax.ShapeDtypeStruct((SUF // 2 + EXTRA, WIDTH), BF)
    shapes = [message] * len(halves) * nq if halves else STATE * nq
    out = call(
        functools.partial(prefix_kernel, nq, nkv, used, held, halves),
        name,
        flops=cost,
        in_specs=[vmem] * (nq + nkv + len(extra)),
        out_specs=[vmem] * len(shapes),
        out_shape=shapes,
    )(*qs, *kvs, *extra)
    return list(out) if halves else [out[i : i + 2] for i in range(0, 2 * nq, 2)]


def combine(parts, length, half, attended):
    tile = HD
    count = SUF // 2 // tile
    row = lax.broadcasted_iota(jnp.int32, (tile, HD), 0)
    for h in range(HQL):
        at = pl.ds(h * HD, HD)
        logs = []
        for part in parts:
            tail = part[SUF // 2 :, at].astype(F32)
            logs.append(
                tail[:count] + tail[count : 2 * count] + tail[2 * count : 3 * count]
            )
        top = functools.reduce(jnp.maximum, logs)
        shares = [jnp.exp2(log - top) for log in logs]
        total = functools.reduce(lambda a, b: a + b, shares)
        shares = [share / total for share in shares]
        for t in range(count):
            rows = pl.ds(t * tile, tile)
            acc = jnp.zeros((tile, HD), F32)
            for share, part in zip(shares, parts):
                wide = jnp.broadcast_to(share[t : t + 1, :], (tile, HD)).T
                acc += wide * part[rows, at].astype(F32)
            live = place_of_row(half * (SUF // 2) + t * tile + row) < length[0]
            attended[rows, at] = jnp.where(live, acc, 0.0).astype(BF)


def output_kernel(n, half, length, *refs):
    parts, weight, outs = refs[:n], refs[n], refs[n + 1 : -2]
    attended, ordered = refs[-2:]

    @pl.when(pl.program_id(0) == 0)
    def _():
        combine(parts, length, half, attended)
        if half == 1:
            xhi = lax.axis_index("xhi")
            groups = [2 * y + x for x in (1 - xhi, xhi) for y in range(4)]
        else:
            y = lax.axis_index("y")
            groups = [2 * lax.rem(y + d, 4) + x for d in range(4) for x in range(2)]
        for i, group in enumerate(groups):
            at = pl.ds(pl.multiple_of(group * PIECE, PIECE), PIECE)
            ordered[pl.ds(i * PIECE, PIECE), :] = attended[at, :]

    rows = outs[0].shape[0]
    for i, out in enumerate(outs):
        out[...] = jnp.dot(
            ordered[pl.ds(i * rows, rows), :], weight[...], preferred_element_type=F32
        ).astype(BF)


def output_half(length, half, parts, weight):
    n = len(parts)
    width = weight.shape[1]
    wide = 1024
    count = 4 if half == 0 else 2
    rows = SUF // 2 // count
    whole = pl.BlockSpec((SUF // 2 + EXTRA, WIDTH), lambda i: (0, 0))
    return call(
        functools.partial(output_kernel, n, half),
        "output_half",
        flops=1 + half * COST,
        grid=(width // wide,),
        in_specs=[pl.BlockSpec(memory_space=pltpu.SMEM)]
        + [whole] * n
        + [pl.BlockSpec((WIDTH, wide), lambda i: (0, i))],
        out_specs=[pl.BlockSpec((rows, wide), lambda i: (0, i))] * count,
        out_shape=[jax.ShapeDtypeStruct((rows, width), BF)] * count,
        scratch_shapes=[pltpu.VMEM((SUF // 2, WIDTH), BF)] * 2,
    )(length, *parts, weight)


def add_up(refs, at=slice(None)):
    return functools.reduce(lambda a, b: a + b, [r[at, :].astype(F32) for r in refs])


def sum_x_kernel(ours, theirs, *outs):
    y = lax.axis_index("y")
    rows = outs[0].shape[0]
    for d, out in enumerate(outs):
        at = pl.ds(pl.multiple_of(lax.rem(y + d, 4) * rows, rows), rows)
        out[...] = add_up([ours, theirs], at).astype(BF)


def sum_x(ours, theirs):
    rows, width = ours.shape
    wide = 1024
    return call(
        sum_x_kernel,
        "sum_x",
        grid=(width // wide,),
        in_specs=[pl.BlockSpec((rows, wide), lambda i: (0, i))] * 2,
        out_specs=[pl.BlockSpec((rows // 4, wide), lambda i: (0, i))] * 4,
        out_shape=[jax.ShapeDtypeStruct((rows // 4, width), BF)] * 4,
    )(ours, theirs)


def sum_y_kernel(n, *refs):
    parts, (theirs, ours) = refs[:n], refs[n:]
    xhi = lax.axis_index("xhi")
    rows = ours.shape[0]
    for part, out in ((1 - xhi, theirs), (xhi, ours)):
        at = pl.ds(pl.multiple_of(part * rows, rows), rows)
        out[...] = add_up(parts, at).astype(BF)


def sum_y(parts):
    rows, width = parts[0].shape
    wide = 1024
    return call(
        functools.partial(sum_y_kernel, len(parts)),
        "sum_y",
        flops=2 * 10**10,
        grid=(width // wide,),
        in_specs=[pl.BlockSpec((rows, wide), lambda i: (0, i))] * len(parts),
        out_specs=[pl.BlockSpec((rows // 2, wide), lambda i: (0, i))] * 2,
        out_shape=[jax.ShapeDtypeStruct((rows // 2, width), BF)] * 2,
    )(*parts)


def finish_kernel(n, *refs):
    upper, lower, out = refs[:n], refs[n:-1], refs[-1]
    rows = upper[0].shape[0]
    out[:rows, :] = add_up(upper).astype(BF)
    out[rows:, :] = add_up(lower).astype(BF)


def finish(upper, lower):
    rows, width = upper[0].shape
    vmem = pl.BlockSpec(memory_space=pltpu.VMEM)
    return call(
        functools.partial(finish_kernel, len(upper)),
        "finish",
        in_specs=[vmem] * (len(upper) + len(lower)),
        out_specs=vmem,
        out_shape=jax.ShapeDtypeStruct((2 * rows, width), BF),
    )(*upper, *lower)


def shift(n, by):
    return [(i, (i + by) % n) for i in range(n)]


def in_order(values, *others):
    return list(lax.optimization_barrier((*values, *others)))[: len(values)]


def body(
    hidden, w_query, w_key, w_value, w_output, prefix_keys, prefix_values, block_slot, suffix_len
):
    slots, block, feats = prefix_keys.shape
    rows = slots * block
    tables = [jnp.asarray(t) for t in suffix_tables()]

    def core(x):
        return lax.ppermute(x, "core", shift(2, 1))

    def along_z(x, by):
        return lax.ppermute(x, "z", shift(4, by))

    sent = prepare(
        block_slot, prefix_keys.reshape(rows, feats), prefix_values.reshape(rows, feats)
    )
    got = [sent[0]] + [lax.ppermute(sent[d], "y", shift(4, d)) for d in (1, 2, 3)]

    (hidden,) = in_order([hidden], sent[0])
    (q,) = project("q", hidden, [w_query], tables)
    q2, q1, q3 = [along_z(q, by) for by in (2, 1, -1)]
    got = in_order(got, q)
    near, far = pack(got)
    near_x = lax.ppermute(near, "xlo", shift(2, 1))
    far_x = lax.ppermute(far, ("xlo", "xhi"), [(0, 3), (3, 0), (1, 2), (2, 1)])
    (hidden,) = in_order([hidden], near)
    k_suffix, v_suffix = project("kv", hidden, [w_key, w_value], tables)
    begun = suffix_attention(suffix_len, q, k_suffix, v_suffix)
    queries = in_order([q2, q1, q3], begun[0])
    near_c = core(in_order([near], *queries)[0])

    near_x, far_x = in_order([near_x, far_x], begun[0])
    far_xx = lax.ppermute(far_x, "xlo", shift(2, 1))
    middle = [near_x, far_x, core(near_x), core(far_x)]
    states = prefix_attention(
        "attend_near",
        in_order(queries, near_x, far_x),
        [near, near_c],
        [2] * 3,
        [None] * 3,
        cost=NEAR_COST,
    )
    states = prefix_attention("attend_middle", queries, middle, [4] * 3, states)
    (far_xx,) = in_order([far_xx], states[0][0])
    final = [far_xx, core(far_xx)]
    sums = []
    for half in range(2):
        sent = prefix_attention("attend_last", queries, final, [2] * 3, states, [half])
        sums.append([along_z(m, back) for m, back in zip(sent, [2, -1, 1])])
        final = in_order(final, sent[0])
    every = [near, near_c, *middle, *final]
    own = prefix_attention("attend_own", [q], every, [8], [begun], [0, 1])
    cut = output_half(suffix_len, 0, in_order(sums[0], own[0]) + [own[0]], w_output)
    sums[1] = in_order(sums[1], cut[0])
    cut = [cut[0]] + [lax.ppermute(cut[d], "y", shift(4, d)) for d in (1, 2, 3)]
    theirs, ours = output_half(suffix_len, 1, sums[1] + [own[1]], w_output)
    theirs = lax.ppermute(theirs, "xhi", shift(2, 1))
    cut = in_order(cut, ours)
    upper_theirs, upper_ours = sum_y(cut)
    upper = [upper_ours, lax.ppermute(upper_theirs, "xhi", shift(2, 1))]
    (theirs,) = in_order([theirs], upper_ours)
    lower = sum_x(ours, theirs)
    lower = [lower[0]] + [lax.ppermute(lower[d], "y", shift(4, d)) for d in (1, 2, 3)]
    return finish(upper, lower)


def solution(mesh):
    fine = Mesh(
        mesh.devices.reshape(2, 4, 2, 4, 2), ("xlo", "z", "core", "y", "xhi")
    )
    pool, head = ("xlo", "z", "core"), ("y", "xhi")
    placed = (
        P(pool, None),
        P(None, head),
        P(None, head),
        P(None, head),
        P(head, None),
        P(pool + head, None, None),
        P(pool + head, None, None),
        P(),
        P(pool),
    )
    return jax.shard_map(
        body, mesh=fine, in_specs=placed, out_specs=P(pool + head, None), check_vma=False
    )
```

```python
import functools
import math

import jax
import jax.numpy as jnp
import numpy as np
from jax import lax
from jax.experimental import pallas as pl
from jax.experimental.pallas import tpu as pltpu
from jax.sharding import Mesh, PartitionSpec as P

HD = 128
HQL = 4
BLOCK = 16
SUF = 512
PREFIX = 8192
WIDTH = HQL * HD
LOG2E = 1.4426950408889634
EXTRA = 16
COST = 5 * 10**9
SUFFIX_COST = 1
NEAR_COST = 10**10
PACK_COST = 4 * 10**9
PIECE = 32
SLABS = 8
BF = jnp.bfloat16
F32 = jnp.float32


def frequencies():
    return np.exp(-math.log(10000.0) * np.arange(HD // 2) * 2.0 / HD)


def suffix_tables():
    angle = (PREFIX + np.arange(SUF))[:, None] * frequencies()[None, :]
    cosine, sine = np.cos(angle), np.sin(angle)
    return (
        np.concatenate([cosine, cosine], axis=1).astype(np.float32),
        np.concatenate([-sine, sine], axis=1).astype(np.float32),
    )


def pieces_of_rows():
    count = SUF // PIECE // 2
    return [
        ((half * count + device) * PIECE, (2 * device + half) * PIECE)
        for half in range(2)
        for device in range(count)
    ]


def place_of_row(row):
    half, inside = row // (SUF // 2), row % (SUF // 2)
    return (2 * (inside // PIECE) + half) * PIECE + inside % PIECE


def call(kernel, name, vmem=24, flops=1, **kwargs):
    return pl.pallas_call(
        kernel,
        name=name,
        cost_estimate=pl.CostEstimate(flops=flops, bytes_accessed=1, transcendentals=0),
        compiler_params=pltpu.CompilerParams(vmem_limit_bytes=vmem * 2**20),
        **kwargs,
    )


def turn(values, cosine, sine):
    return values * cosine + pltpu.roll(values, HD // 2, 1) * sine


def prep_kernel(slots, freq, keys_hbm, values_hbm, *refs):
    outs, (keys, values, sems) = refs[:-3], refs[-3:]
    copies = [
        pltpu.make_async_copy(keys_hbm, keys, sems.at[0]),
        pltpu.make_async_copy(values_hbm, values, sems.at[1]),
    ]
    for copy in copies:
        copy.start()
    y, xhi = lax.axis_index("y"), lax.axis_index("xhi")
    chip = lax.axis_index("xlo") * 4 + lax.axis_index("z")
    device = (chip * 2 + lax.axis_index("core")) * 8 + y * 2 + xhi
    slot0 = device * (keys.shape[0] // BLOCK)
    shape = (slots.shape[0], slots.shape[1])
    block = (
        lax.broadcasted_iota(jnp.int32, shape, 0) * shape[1]
        + lax.broadcasted_iota(jnp.int32, shape, 1)
    ).astype(F32)
    rows = keys.shape[0]
    token = lax.broadcasted_iota(jnp.int32, (rows, HD), 0)
    position = jnp.zeros((rows, HD), F32)
    for i in range(rows // BLOCK):
        owner = jnp.sum(jnp.where(slots[...] == slot0 + i, block, 0.0))
        position = jnp.where(token // BLOCK == i, owner * BLOCK, position)
    position = position + (token % BLOCK).astype(F32)
    angle = position * freq[...]
    cosine = jnp.cos(angle)
    lane = lax.broadcasted_iota(jnp.int32, (rows, HD), 1)
    sine = jnp.sin(angle)
    sine = jnp.where(lane < HD // 2, -sine, sine)
    for kind, copy in enumerate(copies):
        copy.wait()
        for d, out in enumerate(outs):
            target = lax.rem(y + d, 4)
            for part in range(2):
                group = 2 * target + (xhi if part == 0 else 1 - xhi)
                to = pl.ds((part * 2 + kind) * rows, rows)
                for h in range(HQL):
                    at = pl.ds(pl.multiple_of(group * WIDTH + h * HD, HD), HD)
                    if kind == 0:
                        value = turn(keys[:, at].astype(F32), cosine, sine).astype(BF)
                    else:
                        value = values[:, at]
                    out[to, pl.ds(h * HD, HD)] = value


def prepare(block_slot, keys, values):
    rows = keys.shape[0]
    freq = np.tile(frequencies(), 2)[None, :].astype(np.float32)
    vmem = pl.BlockSpec(memory_space=pltpu.VMEM)
    return call(
        prep_kernel,
        "prepare",
        60,
        in_specs=[vmem] * 2
        + [pl.BlockSpec(memory_space=pltpu.HBM)] * 2,
        out_specs=[vmem] * 4,
        out_shape=[jax.ShapeDtypeStruct((4 * rows, WIDTH), BF)] * 4,
        scratch_shapes=[
            pltpu.VMEM(keys.shape, BF),
            pltpu.VMEM(values.shape, BF),
            pltpu.SemaphoreType.DMA((2,)),
        ],
    )(block_slot.reshape(4, -1), jnp.asarray(freq), keys, values)


def project_kernel(kinds, scale, *refs):
    n = len(kinds)
    hidden, weights, tables, outs = refs[0], refs[1 : n + 1], refs[n + 1 : n + 3], refs[n + 3 :]
    outs, (rows, *slabs), turns, sems = outs[:n], outs[n : 2 * n + 1], outs[-3:-1], outs[-1]
    depth = hidden.shape[1]
    deep = depth // SLABS
    copies = []
    for i in range(SLABS):
        at = pl.ds(i * deep, deep)
        slab = [(hidden.at[:, at], rows.at[:, at])]
        slab += [(w.at[at, :], v.at[at, :]) for w, v in zip(weights, slabs)]
        copies.append(
            [
                pltpu.make_async_copy(src, dst, sems.at[i, j])
                for j, (src, dst) in enumerate(slab)
            ]
        )
    copies.append(
        [
            pltpu.make_async_copy(src, dst, sems.at[SLABS, j])
            for j, (src, dst) in enumerate(zip(tables, turns))
        ]
    )
    for group in copies:
        for copy in group:
            copy.start()
    totals = [0.0] * n
    for i in range(SLABS):
        for copy in copies[i]:
            copy.wait()
        at = slice(i * deep, (i + 1) * deep)
        for j, slab in enumerate(slabs):
            totals[j] += jnp.dot(rows[:, at], slab[at, :], preferred_element_type=F32)
    for copy in copies[SLABS]:
        copy.wait()
    cosine, sine = turns
    for kind, out, total in zip(kinds, outs, totals):
        for h in range(HQL):
            at = slice(h * HD, (h + 1) * HD)
            value = total[:, at]
            if kind != "v":
                value = turn(value, cosine[...], sine[...])
            if kind == "q":
                for to, origin in pieces_of_rows():
                    rows_to = pl.ds(to, PIECE)
                    out[rows_to, at] = (value[origin : origin + PIECE] * scale).astype(BF)
            else:
                out[:, at] = value.astype(BF)


def project(kinds, hidden, weights, tables):
    rows, depth = hidden.shape
    n = len(kinds)
    hbm = pl.BlockSpec(memory_space=pltpu.HBM)
    return call(
        functools.partial(project_kernel, kinds, LOG2E / math.sqrt(HD)),
        "project_" + kinds,
        60,
        1,
        in_specs=[hbm] * (n + 3),
        out_specs=[pl.BlockSpec(memory_space=pltpu.VMEM)] * n,
        out_shape=[jax.ShapeDtypeStruct((rows, WIDTH), BF)] * n,
        scratch_shapes=[pltpu.VMEM((rows, depth), BF)]
        + [pltpu.VMEM((depth, WIDTH), BF)] * n
        + [pltpu.VMEM((rows, HD), F32)] * 2
        + [pltpu.SemaphoreType.DMA((SLABS + 1, max(n + 1, 2)))],
    )(hidden, *weights, *tables)


def pack_kernel(n, *refs):
    got, outs = refs[:n], refs[n:]
    rows = got[0].shape[0] // 4
    for part, out in enumerate(outs):
        for kind in range(2):
            for i, piece in enumerate(got):
                at = pl.ds((kind * n + i) * rows, rows)
                out[at, :] = piece[pl.ds((2 * part + kind) * rows, rows), :]


def pack(got):
    rows, width = got[0].shape
    vmem = pl.BlockSpec(memory_space=pltpu.VMEM)
    return call(
        functools.partial(pack_kernel, len(got)),
        "pack",
        flops=PACK_COST,
        in_specs=[vmem] * len(got),
        out_specs=[vmem] * 2,
        out_shape=[jax.ShapeDtypeStruct((len(got) * rows // 2, width), BF)] * 2,
    )(*got)


def widen(v):
    return jnp.concatenate([v, jnp.ones_like(v)], axis=1)


def suffix_kernel(length, q_ref, k_ref, v_ref, sum_ref, top_ref):
    tile = 128
    for t in range(SUF // tile):
        rows, keys = pl.ds(t * tile, tile), (t % 2 + 1) * SUF // 2
        row = place_of_row(t * tile + lax.broadcasted_iota(jnp.int32, (tile, keys), 0))
        column = lax.broadcasted_iota(jnp.int32, (tile, keys), 1)
        mask = (column <= row) & (column < length[0])
        for h in range(HQL):
            head = slice(h * HD, (h + 1) * HD)
            s = lax.dot_general(
                q_ref[rows, head],
                k_ref[:keys, head],
                (((1,), (1,)), ((), ())),
                preferred_element_type=F32,
            )
            s = jnp.where(mask, s, -1e30)
            top = jnp.max(s, axis=1, keepdims=True)
            p = jnp.exp2(s - top).astype(BF)
            sum_ref[rows, 2 * h * HD : 2 * (h + 1) * HD] = jnp.dot(
                p, widen(v_ref[:keys, head]), preferred_element_type=F32
            )
            top_ref[rows, head] = jnp.broadcast_to(top, (tile, HD))


def suffix_attention(length, q, k, v):
    vmem = pl.BlockSpec(memory_space=pltpu.VMEM)
    return call(
        suffix_kernel,
        "suffix_attention",
        flops=SUFFIX_COST,
        in_specs=[pl.BlockSpec(memory_space=pltpu.SMEM)] + [vmem] * 3,
        out_specs=[vmem] * 2,
        out_shape=STATE,
    )(length, q, k, v)


def split_log(log):
    high = log.astype(BF)
    rest = log - high.astype(F32)
    middle = rest.astype(BF)
    return high, middle, (rest - middle.astype(F32)).astype(BF)


def prefix_kernel(nq, nkv, used, held, halves, *refs):
    qs, kvs = refs[:nq], refs[nq : nq + nkv]
    old, at = [], nq + nkv
    for has in held:
        old.append(refs[at : at + 2] if has else None)
        at += 2 * has
    outs = refs[at:]
    half = kvs[0].shape[0] // 2
    tile = SUF // 2

    def one_tile(h, r, rows, out=None):
        head = slice(h * HD, (h + 1) * HD)
        wide = slice(2 * h * HD, 2 * (h + 1) * HD)
        n = used[r]
        k = jnp.concatenate([kv[:half, head] for kv in kvs[:n]], axis=0)
        v = jnp.concatenate([kv[half:, head] for kv in kvs[:n]], axis=0)
        s = lax.dot_general(
            qs[r][rows, head],
            k,
            (((1,), (1,)), ((), ())),
            preferred_element_type=F32,
        )
        top = jnp.broadcast_to(jnp.max(s, axis=1, keepdims=True), (tile, HD))
        if old[r] is not None:
            before = old[r][1][rows, head]
            top = jnp.maximum(before, top)
        p = jnp.exp2(s - jnp.concatenate([top] * (n * half // HD), axis=1)).astype(BF)
        both = jnp.dot(p, widen(v), preferred_element_type=F32)
        if old[r] is not None:
            shrink = jnp.exp2(before - top)
            both += jnp.concatenate([shrink] * 2, axis=1) * old[r][0][rows, wide]
        if not halves:
            outs[2 * r][rows, wide] = both
            outs[2 * r + 1][rows, head] = top
            return
        acc, total = both[:, :HD], both[:, HD:]
        out[:tile, head] = (acc / total).astype(BF)
        log = top + jnp.log2(total)
        logs = [log[i : i + HD].T[:1] for i in range(0, tile, HD)]
        rest = jnp.zeros((EXTRA - 3 * len(logs), HD), BF)
        parts = split_log(jnp.concatenate(logs, axis=0))
        out[tile:, head] = jnp.concatenate([*parts, rest], axis=0)

    if not halves:

        @pl.loop(0, SUF // tile)
        def _(t):
            rows = pl.ds(pl.multiple_of(t * tile, tile), tile)
            for h in range(HQL):
                for r in range(nq):
                    one_tile(h, r, rows)

        return
    for h in range(HQL):
        for r in range(nq):
            for i, t in enumerate(halves):
                out = outs[r * len(halves) + i]
                one_tile(h, r, pl.ds(t * tile, tile), out)


STATE = [
    jax.ShapeDtypeStruct((SUF, 2 * WIDTH), F32),
    jax.ShapeDtypeStruct((SUF, WIDTH), F32),
]


def prefix_attention(name, qs, kvs, used, states, halves=(), cost=1):
    nq, nkv = len(qs), len(kvs)
    held = [state is not None for state in states]
    extra = [x for state in states if state is not None for x in state]
    vmem = pl.BlockSpec(memory_space=pltpu.VMEM)
    message = jax.ShapeDtypeStruct((SUF // 2 + EXTRA, WIDTH), BF)
    shapes = [message] * len(halves) * nq if halves else STATE * nq
    out = call(
        functools.partial(prefix_kernel, nq, nkv, used, held, halves),
        name,
        flops=cost,
        in_specs=[vmem] * (nq + nkv + len(extra)),
        out_specs=[vmem] * len(shapes),
        out_shape=shapes,
    )(*qs, *kvs, *extra)
    return list(out) if halves else [out[i : i + 2] for i in range(0, 2 * nq, 2)]


def combine(parts, length, half, attended):
    tile = HD
    count = SUF // 2 // tile
    row = lax.broadcasted_iota(jnp.int32, (tile, HD), 0)
    for h in range(HQL):
        at = pl.ds(h * HD, HD)
        logs = []
        for part in parts:
            tail = part[SUF // 2 :, at].astype(F32)
            logs.append(
                tail[:count] + tail[count : 2 * count] + tail[2 * count : 3 * count]
            )
        top = functools.reduce(jnp.maximum, logs)
        shares = [jnp.exp2(log - top) for log in logs]
        total = functools.reduce(lambda a, b: a + b, shares)
        shares = [share / total for share in shares]
        for t in range(count):
            rows = pl.ds(t * tile, tile)
            acc = jnp.zeros((tile, HD), F32)
            for share, part in zip(shares, parts):
                wide = jnp.broadcast_to(share[t : t + 1, :], (tile, HD)).T
                acc += wide * part[rows, at].astype(F32)
            live = place_of_row(half * (SUF // 2) + t * tile + row) < length[0]
            attended[rows, at] = jnp.where(live, acc, 0.0).astype(BF)


def output_kernel(n, half, length, *refs):
    parts, weight, outs = refs[:n], refs[n], refs[n + 1 : -2]
    attended, ordered = refs[-2:]

    @pl.when(pl.program_id(0) == 0)
    def _():
        combine(parts, length, half, attended)
        if half == 1:
            xhi = lax.axis_index("xhi")
            groups = [2 * y + x for x in (1 - xhi, xhi) for y in range(4)]
        else:
            y = lax.axis_index("y")
            groups = [2 * lax.rem(y + d, 4) + x for d in range(4) for x in range(2)]
        for i, group in enumerate(groups):
            at = pl.ds(pl.multiple_of(group * PIECE, PIECE), PIECE)
            ordered[pl.ds(i * PIECE, PIECE), :] = attended[at, :]

    rows = outs[0].shape[0]
    for i, out in enumerate(outs):
        out[...] = jnp.dot(
            ordered[pl.ds(i * rows, rows), :], weight[...], preferred_element_type=F32
        ).astype(BF)


def output_half(length, half, parts, weight):
    n = len(parts)
    width = weight.shape[1]
    wide = 1024
    count = 4 if half == 0 else 2
    rows = SUF // 2 // count
    whole = pl.BlockSpec((SUF // 2 + EXTRA, WIDTH), lambda i: (0, 0))
    return call(
        functools.partial(output_kernel, n, half),
        "output_half",
        flops=1 + half * COST,
        grid=(width // wide,),
        in_specs=[pl.BlockSpec(memory_space=pltpu.SMEM)]
        + [whole] * n
        + [pl.BlockSpec((WIDTH, wide), lambda i: (0, i))],
        out_specs=[pl.BlockSpec((rows, wide), lambda i: (0, i))] * count,
        out_shape=[jax.ShapeDtypeStruct((rows, width), BF)] * count,
        scratch_shapes=[pltpu.VMEM((SUF // 2, WIDTH), BF)] * 2,
    )(length, *parts, weight)


def add_up(refs, at=slice(None)):
    return functools.reduce(lambda a, b: a + b, [r[at, :].astype(F32) for r in refs])


def sum_x_kernel(ours, theirs, *outs):
    y = lax.axis_index("y")
    rows = outs[0].shape[0]
    for d, out in enumerate(outs):
        at = pl.ds(pl.multiple_of(lax.rem(y + d, 4) * rows, rows), rows)
        out[...] = add_up([ours, theirs], at).astype(BF)


def sum_x(ours, theirs):
    rows, width = ours.shape
    wide = 1024
    return call(
        sum_x_kernel,
        "sum_x",
        grid=(width // wide,),
        in_specs=[pl.BlockSpec((rows, wide), lambda i: (0, i))] * 2,
        out_specs=[pl.BlockSpec((rows // 4, wide), lambda i: (0, i))] * 4,
        out_shape=[jax.ShapeDtypeStruct((rows // 4, width), BF)] * 4,
    )(ours, theirs)


def sum_y_kernel(n, *refs):
    parts, (theirs, ours) = refs[:n], refs[n:]
    xhi = lax.axis_index("xhi")
    rows = ours.shape[0]
    for part, out in ((1 - xhi, theirs), (xhi, ours)):
        at = pl.ds(pl.multiple_of(part * rows, rows), rows)
        out[...] = add_up(parts, at).astype(BF)


def sum_y(parts):
    rows, width = parts[0].shape
    wide = 1024
    return call(
        functools.partial(sum_y_kernel, len(parts)),
        "sum_y",
        flops=2 * 10**10,
        grid=(width // wide,),
        in_specs=[pl.BlockSpec((rows, wide), lambda i: (0, i))] * len(parts),
        out_specs=[pl.BlockSpec((rows // 2, wide), lambda i: (0, i))] * 2,
        out_shape=[jax.ShapeDtypeStruct((rows // 2, width), BF)] * 2,
    )(*parts)


def finish_kernel(n, *refs):
    upper, lower, out = refs[:n], refs[n:-1], refs[-1]
    rows = upper[0].shape[0]
    out[:rows, :] = add_up(upper).astype(BF)
    out[rows:, :] = add_up(lower).astype(BF)


def finish(upper, lower):
    rows, width = upper[0].shape
    vmem = pl.BlockSpec(memory_space=pltpu.VMEM)
    return call(
        functools.partial(finish_kernel, len(upper)),
        "finish",
        in_specs=[vmem] * (len(upper) + len(lower)),
        out_specs=vmem,
        out_shape=jax.ShapeDtypeStruct((2 * rows, width), BF),
    )(*upper, *lower)


def shift(n, by):
    return [(i, (i + by) % n) for i in range(n)]


def in_order(values, *others):
    return list(lax.optimization_barrier((*values, *others)))[: len(values)]


def body(
    hidden, w_query, w_key, w_value, w_output, prefix_keys, prefix_values, block_slot, suffix_len
):
    slots, block, feats = prefix_keys.shape
    rows = slots * block
    tables = [jnp.asarray(t) for t in suffix_tables()]

    def core(x):
        return lax.ppermute(x, "core", shift(2, 1))

    def along_z(x, by):
        return lax.ppermute(x, "z", shift(4, by))

    sent = prepare(
        block_slot, prefix_keys.reshape(rows, feats), prefix_values.reshape(rows, feats)
    )
    got = [sent[0]] + [lax.ppermute(sent[d], "y", shift(4, d)) for d in (1, 2, 3)]

    (hidden,) = in_order([hidden], sent[0])
    (q,) = project("q", hidden, [w_query], tables)
    q1, q3, q2 = [along_z(q, by) for by in (1, -1, 2)]
    got = in_order(got, q)
    near, far = pack(got)
    near_x = lax.ppermute(near, "xlo", shift(2, 1))
    far_x = lax.ppermute(far, ("xlo", "xhi"), [(0, 3), (3, 0), (1, 2), (2, 1)])
    (hidden,) = in_order([hidden], near)
    k_suffix, v_suffix = project("kv", hidden, [w_key, w_value], tables)
    q1, q3 = in_order([q1, q3], k_suffix)
    near_c = core(in_order([near], q1, q3)[0])

    near_x, far_x = in_order([near_x, far_x], k_suffix)
    far_xx = lax.ppermute(far_x, "xlo", shift(2, 1))
    middle = [near_x, far_x, core(near_x), core(far_x)]
    state1, state3 = prefix_attention(
        "attend_near",
        in_order([q1, q3], near_x, far_x),
        [near, near_c],
        [2] * 2,
        [None] * 2,
        cost=NEAR_COST,
    )
    state1, state3 = prefix_attention(
        "attend_middle", [q1, q3], middle, [4] * 2, [state1, state3]
    )
    (q2,) = in_order([q2], state1[0])
    (state2,) = prefix_attention(
        "attend_two", [q2], [near, near_c, *middle], [6], [None]
    )
    queries, states = [q2, q1, q3], [state2, state1, state3]
    (far_xx,) = in_order([far_xx], state2[0])
    final = [far_xx, core(far_xx)]
    sums = []
    for half in range(2):
        sent = prefix_attention("attend_last", queries, final, [2] * 3, states, [half])
        sums.append([along_z(m, back) for m, back in zip(sent, [2, -1, 1])])
        final = in_order(final, sent[0])
    (k_suffix,) = in_order([k_suffix], final[0])
    begun = suffix_attention(suffix_len, q, k_suffix, v_suffix)
    every = [near, near_c, *middle, *final]
    own = prefix_attention("attend_own", [q], every, [8], [begun], [0, 1])
    cut = output_half(suffix_len, 0, in_order(sums[0], own[0]) + [own[0]], w_output)
    sums[1] = in_order(sums[1], cut[0])
    cut = [cut[0]] + [lax.ppermute(cut[d], "y", shift(4, d)) for d in (1, 2, 3)]
    theirs, ours = output_half(suffix_len, 1, sums[1] + [own[1]], w_output)
    theirs = lax.ppermute(theirs, "xhi", shift(2, 1))
    cut = in_order(cut, ours)
    upper_theirs, upper_ours = sum_y(cut)
    upper = [upper_ours, lax.ppermute(upper_theirs, "xhi", shift(2, 1))]
    (theirs,) = in_order([theirs], upper_ours)
    lower = sum_x(ours, theirs)
    lower = [lower[0]] + [lax.ppermute(lower[d], "y", shift(4, d)) for d in (1, 2, 3)]
    return finish(upper, lower)


def solution(mesh):
    fine = Mesh(
        mesh.devices.reshape(2, 4, 2, 4, 2), ("xlo", "z", "core", "y", "xhi")
    )
    pool, head = ("xlo", "z", "core"), ("y", "xhi")
    placed = (
        P(pool, None),
        P(None, head),
        P(None, head),
        P(None, head),
        P(head, None),
        P(pool + head, None, None),
        P(pool + head, None, None),
        P(),
        P(pool),
    )
    return jax.shard_map(
        body, mesh=fine, in_specs=placed, out_specs=P(pool + head, None), check_vma=False
    )
```

```python
import functools
import math

import jax
import jax.numpy as jnp
import numpy as np
from jax import lax
from jax.experimental import pallas as pl
from jax.experimental.pallas import tpu as pltpu
from jax.sharding import Mesh, PartitionSpec as P

HD = 128
HQL = 4
BLOCK = 16
SUF = 512
PREFIX = 8192
WIDTH = HQL * HD
LOG2E = 1.4426950408889634
EXTRA = 16
COST = 5 * 10**9
SUFFIX_COST = 1
NEAR_COST = 10**10
PACK_COST = 4 * 10**9
PIECE = 32
SLABS = 8
BF = jnp.bfloat16
F32 = jnp.float32


def frequencies():
    return np.exp(-math.log(10000.0) * np.arange(HD // 2) * 2.0 / HD)


def suffix_tables():
    angle = (PREFIX + np.arange(SUF))[:, None] * frequencies()[None, :]
    cosine, sine = np.cos(angle), np.sin(angle)
    return (
        np.concatenate([cosine, cosine], axis=1).astype(np.float32),
        np.concatenate([-sine, sine], axis=1).astype(np.float32),
    )


def pieces_of_rows():
    count = SUF // PIECE // 2
    return [
        ((half * count + device) * PIECE, (2 * device + half) * PIECE)
        for half in range(2)
        for device in range(count)
    ]


def place_of_row(row):
    half, inside = row // (SUF // 2), row % (SUF // 2)
    return (2 * (inside // PIECE) + half) * PIECE + inside % PIECE


def call(kernel, name, vmem=24, flops=1, **kwargs):
    return pl.pallas_call(
        kernel,
        name=name,
        cost_estimate=pl.CostEstimate(flops=flops, bytes_accessed=1, transcendentals=0),
        compiler_params=pltpu.CompilerParams(vmem_limit_bytes=vmem * 2**20),
        **kwargs,
    )


def turn(values, cosine, sine):
    return values * cosine + pltpu.roll(values, HD // 2, 1) * sine


def prep_kernel(slots, freq, keys_hbm, values_hbm, *refs):
    outs, (keys, values, sems) = refs[:-3], refs[-3:]
    copies = [
        pltpu.make_async_copy(keys_hbm, keys, sems.at[0]),
        pltpu.make_async_copy(values_hbm, values, sems.at[1]),
    ]
    for copy in copies:
        copy.start()
    y, xhi = lax.axis_index("y"), lax.axis_index("xhi")
    chip = lax.axis_index("xlo") * 4 + lax.axis_index("z")
    device = (chip * 2 + lax.axis_index("core")) * 8 + y * 2 + xhi
    slot0 = device * (keys.shape[0] // BLOCK)
    shape = (slots.shape[0], slots.shape[1])
    block = (
        lax.broadcasted_iota(jnp.int32, shape, 0) * shape[1]
        + lax.broadcasted_iota(jnp.int32, shape, 1)
    ).astype(F32)
    rows = keys.shape[0]
    token = lax.broadcasted_iota(jnp.int32, (rows, HD), 0)
    position = jnp.zeros((rows, HD), F32)
    for i in range(rows // BLOCK):
        owner = jnp.sum(jnp.where(slots[...] == slot0 + i, block, 0.0))
        position = jnp.where(token // BLOCK == i, owner * BLOCK, position)
    position = position + (token % BLOCK).astype(F32)
    angle = position * freq[...]
    cosine = jnp.cos(angle)
    lane = lax.broadcasted_iota(jnp.int32, (rows, HD), 1)
    sine = jnp.sin(angle)
    sine = jnp.where(lane < HD // 2, -sine, sine)
    for kind, copy in enumerate(copies):
        copy.wait()
        for d, out in enumerate(outs):
            target = lax.rem(y + d, 4)
            for part in range(2):
                group = 2 * target + (xhi if part == 0 else 1 - xhi)
                to = pl.ds((part * 2 + kind) * rows, rows)
                for h in range(HQL):
                    at = pl.ds(pl.multiple_of(group * WIDTH + h * HD, HD), HD)
                    if kind == 0:
                        value = turn(keys[:, at].astype(F32), cosine, sine).astype(BF)
                    else:
                        value = values[:, at]
                    out[to, pl.ds(h * HD, HD)] = value


def prepare(block_slot, keys, values):
    rows = keys.shape[0]
    freq = np.tile(frequencies(), 2)[None, :].astype(np.float32)
    vmem = pl.BlockSpec(memory_space=pltpu.VMEM)
    return call(
        prep_kernel,
        "prepare",
        60,
        in_specs=[vmem] * 2
        + [pl.BlockSpec(memory_space=pltpu.HBM)] * 2,
        out_specs=[vmem] * 4,
        out_shape=[jax.ShapeDtypeStruct((4 * rows, WIDTH), BF)] * 4,
        scratch_shapes=[
            pltpu.VMEM(keys.shape, BF),
            pltpu.VMEM(values.shape, BF),
            pltpu.SemaphoreType.DMA((2,)),
        ],
    )(block_slot.reshape(4, -1), jnp.asarray(freq), keys, values)


def project_kernel(kinds, scale, *refs):
    n = len(kinds)
    hidden, weights, tables, outs = refs[0], refs[1 : n + 1], refs[n + 1 : n + 3], refs[n + 3 :]
    outs, (rows, *slabs), turns, sems = outs[:n], outs[n : 2 * n + 1], outs[-3:-1], outs[-1]
    depth = hidden.shape[1]
    deep = depth // SLABS
    copies = []
    for i in range(SLABS):
        at = pl.ds(i * deep, deep)
        slab = [(hidden.at[:, at], rows.at[:, at])]
        slab += [(w.at[at, :], v.at[at, :]) for w, v in zip(weights, slabs)]
        copies.append(
            [
                pltpu.make_async_copy(src, dst, sems.at[i, j])
                for j, (src, dst) in enumerate(slab)
            ]
        )
    copies.append(
        [
            pltpu.make_async_copy(src, dst, sems.at[SLABS, j])
            for j, (src, dst) in enumerate(zip(tables, turns))
        ]
    )
    for group in copies:
        for copy in group:
            copy.start()
    totals = [0.0] * n
    for i in range(SLABS):
        for copy in copies[i]:
            copy.wait()
        at = slice(i * deep, (i + 1) * deep)
        for j, slab in enumerate(slabs):
            totals[j] += jnp.dot(rows[:, at], slab[at, :], preferred_element_type=F32)
    for copy in copies[SLABS]:
        copy.wait()
    cosine, sine = turns
    for kind, out, total in zip(kinds, outs, totals):
        for h in range(HQL):
            at = slice(h * HD, (h + 1) * HD)
            value = total[:, at]
            if kind != "v":
                value = turn(value, cosine[...], sine[...])
            if kind == "q":
                for to, origin in pieces_of_rows():
                    rows_to = pl.ds(to, PIECE)
                    out[rows_to, at] = (value[origin : origin + PIECE] * scale).astype(BF)
            else:
                out[:, at] = value.astype(BF)


def project(kinds, hidden, weights, tables):
    rows, depth = hidden.shape
    n = len(kinds)
    hbm = pl.BlockSpec(memory_space=pltpu.HBM)
    return call(
        functools.partial(project_kernel, kinds, LOG2E / math.sqrt(HD)),
        "project_" + kinds,
        60,
        1,
        in_specs=[hbm] * (n + 3),
        out_specs=[pl.BlockSpec(memory_space=pltpu.VMEM)] * n,
        out_shape=[jax.ShapeDtypeStruct((rows, WIDTH), BF)] * n,
        scratch_shapes=[pltpu.VMEM((rows, depth), BF)]
        + [pltpu.VMEM((depth, WIDTH), BF)] * n
        + [pltpu.VMEM((rows, HD), F32)] * 2
        + [pltpu.SemaphoreType.DMA((SLABS + 1, max(n + 1, 2)))],
    )(hidden, *weights, *tables)


def pack_kernel(n, *refs):
    got, outs = refs[:n], refs[n:]
    rows = got[0].shape[0] // 4
    for part, out in enumerate(outs):
        for kind in range(2):
            for i, piece in enumerate(got):
                at = pl.ds((kind * n + i) * rows, rows)
                out[at, :] = piece[pl.ds((2 * part + kind) * rows, rows), :]


def pack(got):
    rows, width = got[0].shape
    vmem = pl.BlockSpec(memory_space=pltpu.VMEM)
    return call(
        functools.partial(pack_kernel, len(got)),
        "pack",
        flops=PACK_COST,
        in_specs=[vmem] * len(got),
        out_specs=[vmem] * 2,
        out_shape=[jax.ShapeDtypeStruct((len(got) * rows // 2, width), BF)] * 2,
    )(*got)


def widen(v):
    return jnp.concatenate([v, jnp.ones_like(v)], axis=1)


def suffix_kernel(length, q_ref, k_ref, v_ref, sum_ref, top_ref):
    tile = 128
    for t in range(SUF // tile):
        rows, keys = pl.ds(t * tile, tile), (t % 2 + 1) * SUF // 2
        row = place_of_row(t * tile + lax.broadcasted_iota(jnp.int32, (tile, keys), 0))
        column = lax.broadcasted_iota(jnp.int32, (tile, keys), 1)
        mask = (column <= row) & (column < length[0])
        for h in range(HQL):
            head = slice(h * HD, (h + 1) * HD)
            s = lax.dot_general(
                q_ref[rows, head],
                k_ref[:keys, head],
                (((1,), (1,)), ((), ())),
                preferred_element_type=F32,
            )
            s = jnp.where(mask, s, -1e30)
            top = jnp.max(s, axis=1, keepdims=True)
            p = jnp.exp2(s - top).astype(BF)
            sum_ref[rows, 2 * h * HD : 2 * (h + 1) * HD] = jnp.dot(
                p, widen(v_ref[:keys, head]), preferred_element_type=F32
            )
            top_ref[rows, head] = jnp.broadcast_to(top, (tile, HD))


def suffix_attention(length, q, k, v):
    vmem = pl.BlockSpec(memory_space=pltpu.VMEM)
    return call(
        suffix_kernel,
        "suffix_attention",
        flops=SUFFIX_COST,
        in_specs=[pl.BlockSpec(memory_space=pltpu.SMEM)] + [vmem] * 3,
        out_specs=[vmem] * 2,
        out_shape=STATE,
    )(length, q, k, v)


def split_log(log):
    high = log.astype(BF)
    rest = log - high.astype(F32)
    middle = rest.astype(BF)
    return high, middle, (rest - middle.astype(F32)).astype(BF)


def prefix_kernel(nq, nkv, used, held, halves, *refs):
    qs, kvs = refs[:nq], refs[nq : nq + nkv]
    old, at = [], nq + nkv
    for has in held:
        old.append(refs[at : at + 2] if has else None)
        at += 2 * has
    outs = refs[at:]
    half = kvs[0].shape[0] // 2
    tile = SUF // 2

    def one_tile(h, r, rows, out=None):
        head = slice(h * HD, (h + 1) * HD)
        wide = slice(2 * h * HD, 2 * (h + 1) * HD)
        n = used[r]
        k = jnp.concatenate([kv[:half, head] for kv in kvs[:n]], axis=0)
        v = jnp.concatenate([kv[half:, head] for kv in kvs[:n]], axis=0)
        s = lax.dot_general(
            qs[r][rows, head],
            k,
            (((1,), (1,)), ((), ())),
            preferred_element_type=F32,
        )
        top = jnp.broadcast_to(jnp.max(s, axis=1, keepdims=True), (tile, HD))
        if old[r] is not None:
            before = old[r][1][rows, head]
            top = jnp.maximum(before, top)
        p = jnp.exp2(s - jnp.concatenate([top] * (n * half // HD), axis=1)).astype(BF)
        both = jnp.dot(p, widen(v), preferred_element_type=F32)
        if old[r] is not None:
            shrink = jnp.exp2(before - top)
            both += jnp.concatenate([shrink] * 2, axis=1) * old[r][0][rows, wide]
        if not halves:
            outs[2 * r][rows, wide] = both
            outs[2 * r + 1][rows, head] = top
            return
        acc, total = both[:, :HD], both[:, HD:]
        out[:tile, head] = (acc / total).astype(BF)
        log = top + jnp.log2(total)
        logs = [log[i : i + HD].T[:1] for i in range(0, tile, HD)]
        rest = jnp.zeros((EXTRA - 3 * len(logs), HD), BF)
        parts = split_log(jnp.concatenate(logs, axis=0))
        out[tile:, head] = jnp.concatenate([*parts, rest], axis=0)

    if not halves:

        @pl.loop(0, SUF // tile)
        def _(t):
            rows = pl.ds(pl.multiple_of(t * tile, tile), tile)
            for h in range(HQL):
                for r in range(nq):
                    one_tile(h, r, rows)

        return
    for h in range(HQL):
        for r in range(nq):
            for i, t in enumerate(halves):
                out = outs[r * len(halves) + i]
                one_tile(h, r, pl.ds(t * tile, tile), out)


STATE = [
    jax.ShapeDtypeStruct((SUF, 2 * WIDTH), F32),
    jax.ShapeDtypeStruct((SUF, WIDTH), F32),
]


def prefix_attention(name, qs, kvs, used, states, halves=(), cost=1):
    nq, nkv = len(qs), len(kvs)
    held = [state is not None for state in states]
    extra = [x for state in states if state is not None for x in state]
    vmem = pl.BlockSpec(memory_space=pltpu.VMEM)
    message = jax.ShapeDtypeStruct((SUF // 2 + EXTRA, WIDTH), BF)
    shapes = [message] * len(halves) * nq if halves else STATE * nq
    out = call(
        functools.partial(prefix_kernel, nq, nkv, used, held, halves),
        name,
        flops=cost,
        in_specs=[vmem] * (nq + nkv + len(extra)),
        out_specs=[vmem] * len(shapes),
        out_shape=shapes,
    )(*qs, *kvs, *extra)
    return list(out) if halves else [out[i : i + 2] for i in range(0, 2 * nq, 2)]


def combine(parts, length, half, attended):
    tile = HD
    count = SUF // 2 // tile
    row = lax.broadcasted_iota(jnp.int32, (tile, HD), 0)
    for h in range(HQL):
        at = pl.ds(h * HD, HD)
        logs = []
        for part in parts:
            tail = part[SUF // 2 :, at].astype(F32)
            logs.append(
                tail[:count] + tail[count : 2 * count] + tail[2 * count : 3 * count]
            )
        top = functools.reduce(jnp.maximum, logs)
        shares = [jnp.exp2(log - top) for log in logs]
        total = functools.reduce(lambda a, b: a + b, shares)
        shares = [share / total for share in shares]
        for t in range(count):
            rows = pl.ds(t * tile, tile)
            acc = jnp.zeros((tile, HD), F32)
            for share, part in zip(shares, parts):
                wide = jnp.broadcast_to(share[t : t + 1, :], (tile, HD)).T
                acc += wide * part[rows, at].astype(F32)
            live = place_of_row(half * (SUF // 2) + t * tile + row) < length[0]
            attended[rows, at] = jnp.where(live, acc, 0.0).astype(BF)


def output_kernel(n, half, length, *refs):
    parts, weight, outs = refs[:n], refs[n], refs[n + 1 : -2]
    attended, ordered = refs[-2:]

    @pl.when(pl.program_id(0) == 0)
    def _():
        combine(parts, length, half, attended)
        if half == 1:
            xhi = lax.axis_index("xhi")
            groups = [2 * y + x for x in (1 - xhi, xhi) for y in range(4)]
        else:
            y = lax.axis_index("y")
            groups = [2 * lax.rem(y + d, 4) + x for d in range(4) for x in range(2)]
        for i, group in enumerate(groups):
            at = pl.ds(pl.multiple_of(group * PIECE, PIECE), PIECE)
            ordered[pl.ds(i * PIECE, PIECE), :] = attended[at, :]

    rows = outs[0].shape[0]
    for i, out in enumerate(outs):
        out[...] = jnp.dot(
            ordered[pl.ds(i * rows, rows), :], weight[...], preferred_element_type=F32
        ).astype(BF)


def output_half(length, half, parts, weight):
    n = len(parts)
    width = weight.shape[1]
    wide = 1024
    count = 4 if half == 0 else 2
    rows = SUF // 2 // count
    whole = pl.BlockSpec((SUF // 2 + EXTRA, WIDTH), lambda i: (0, 0))
    return call(
        functools.partial(output_kernel, n, half),
        "output_half",
        flops=1 + half * COST,
        grid=(width // wide,),
        in_specs=[pl.BlockSpec(memory_space=pltpu.SMEM)]
        + [whole] * n
        + [pl.BlockSpec((WIDTH, wide), lambda i: (0, i))],
        out_specs=[pl.BlockSpec((rows, wide), lambda i: (0, i))] * count,
        out_shape=[jax.ShapeDtypeStruct((rows, width), BF)] * count,
        scratch_shapes=[pltpu.VMEM((SUF // 2, WIDTH), BF)] * 2,
    )(length, *parts, weight)


def add_up(refs, at=slice(None)):
    return functools.reduce(lambda a, b: a + b, [r[at, :].astype(F32) for r in refs])


def sum_x_kernel(ours, theirs, *outs):
    y = lax.axis_index("y")
    rows = outs[0].shape[0]
    for d, out in enumerate(outs):
        at = pl.ds(pl.multiple_of(lax.rem(y + d, 4) * rows, rows), rows)
        out[...] = add_up([ours, theirs], at).astype(BF)


def sum_x(ours, theirs):
    rows, width = ours.shape
    wide = 1024
    return call(
        sum_x_kernel,
        "sum_x",
        grid=(width // wide,),
        in_specs=[pl.BlockSpec((rows, wide), lambda i: (0, i))] * 2,
        out_specs=[pl.BlockSpec((rows // 4, wide), lambda i: (0, i))] * 4,
        out_shape=[jax.ShapeDtypeStruct((rows // 4, width), BF)] * 4,
    )(ours, theirs)


def sum_y_kernel(n, *refs):
    parts, (theirs, ours) = refs[:n], refs[n:]
    xhi = lax.axis_index("xhi")
    rows = ours.shape[0]
    for part, out in ((1 - xhi, theirs), (xhi, ours)):
        at = pl.ds(pl.multiple_of(part * rows, rows), rows)
        out[...] = add_up(parts, at).astype(BF)


def sum_y(parts):
    rows, width = parts[0].shape
    wide = 1024
    return call(
        functools.partial(sum_y_kernel, len(parts)),
        "sum_y",
        flops=2 * 10**10,
        grid=(width // wide,),
        in_specs=[pl.BlockSpec((rows, wide), lambda i: (0, i))] * len(parts),
        out_specs=[pl.BlockSpec((rows // 2, wide), lambda i: (0, i))] * 2,
        out_shape=[jax.ShapeDtypeStruct((rows // 2, width), BF)] * 2,
    )(*parts)


def finish_kernel(n, *refs):
    upper, lower, out = refs[:n], refs[n:-1], refs[-1]
    rows = upper[0].shape[0]
    out[:rows, :] = add_up(upper).astype(BF)
    out[rows:, :] = add_up(lower).astype(BF)


def finish(upper, lower):
    rows, width = upper[0].shape
    vmem = pl.BlockSpec(memory_space=pltpu.VMEM)
    return call(
        functools.partial(finish_kernel, len(upper)),
        "finish",
        in_specs=[vmem] * (len(upper) + len(lower)),
        out_specs=vmem,
        out_shape=jax.ShapeDtypeStruct((2 * rows, width), BF),
    )(*upper, *lower)


def shift(n, by):
    return [(i, (i + by) % n) for i in range(n)]


def in_order(values, *others):
    return list(lax.optimization_barrier((*values, *others)))[: len(values)]


def body(
    hidden, w_query, w_key, w_value, w_output, prefix_keys, prefix_values, block_slot, suffix_len
):
    slots, block, feats = prefix_keys.shape
    rows = slots * block
    tables = [jnp.asarray(t) for t in suffix_tables()]

    def core(x):
        return lax.ppermute(x, "core", shift(2, 1))

    def along_z(x, by):
        return lax.ppermute(x, "z", shift(4, by))

    sent = prepare(
        block_slot, prefix_keys.reshape(rows, feats), prefix_values.reshape(rows, feats)
    )
    got = [sent[0]] + [lax.ppermute(sent[d], "y", shift(4, d)) for d in (1, 2, 3)]

    (hidden,) = in_order([hidden], sent[0])
    (q,) = project("q", hidden, [w_query], tables)
    q1, q3, q2 = [along_z(q, by) for by in (1, -1, 2)]
    got = in_order(got, q)
    near, far = pack(got)
    near_x = lax.ppermute(near, "xlo", shift(2, 1))
    far_x = lax.ppermute(far, ("xlo", "xhi"), [(0, 3), (3, 0), (1, 2), (2, 1)])
    (hidden,) = in_order([hidden], near)
    k_suffix, v_suffix = project("kv", hidden, [w_key, w_value], tables)
    q1, q3 = in_order([q1, q3], k_suffix)
    near_c = core(in_order([near], q1, q3)[0])

    near_x, far_x = in_order([near_x, far_x], k_suffix)
    far_xx = lax.ppermute(far_x, "xlo", shift(2, 1))
    middle = [near_x, far_x, core(near_x), core(far_x)]
    state1, state3 = prefix_attention(
        "attend_near",
        in_order([q1, q3], near_x, far_x),
        [near, near_c],
        [2] * 2,
        [None] * 2,
        cost=NEAR_COST,
    )
    state1, state3 = prefix_attention(
        "attend_middle", [q1, q3], middle, [4] * 2, [state1, state3]
    )
    (q2,) = in_order([q2], state1[0])
    (state2,) = prefix_attention(
        "attend_two", [q2], [near, near_c, *middle], [6], [None]
    )
    queries, states = [q1, q2, q3], [state1, state2, state3]
    (far_xx,) = in_order([far_xx], state2[0])
    final = [far_xx, core(far_xx)]
    (k_suffix,) = in_order([k_suffix], far_xx)
    begun = suffix_attention(suffix_len, q, k_suffix, v_suffix)
    final[1:] = in_order(final[1:], begun[0])
    sums = []
    for half in range(2):
        sent = prefix_attention("attend_last", queries, final, [2] * 3, states, [half])
        sums.append([along_z(m, back) for m, back in zip(sent, [-1, 2, 1])])
        final = in_order(final, sent[0])
    every = [near, near_c, *middle, *final]
    own = prefix_attention("attend_own", [q], every, [8], [begun], [0, 1])
    cut = output_half(suffix_len, 0, in_order(sums[0], own[0]) + [own[0]], w_output)
    sums[1] = in_order(sums[1], cut[0])
    cut = [cut[0]] + [lax.ppermute(cut[d], "y", shift(4, d)) for d in (1, 2, 3)]
    theirs, ours = output_half(suffix_len, 1, sums[1] + [own[1]], w_output)
    theirs = lax.ppermute(theirs, "xhi", shift(2, 1))
    cut = in_order(cut, ours)
    upper_theirs, upper_ours = sum_y(cut)
    upper = [upper_ours, lax.ppermute(upper_theirs, "xhi", shift(2, 1))]
    (theirs,) = in_order([theirs], upper_ours)
    lower = sum_x(ours, theirs)
    lower = [lower[0]] + [lax.ppermute(lower[d], "y", shift(4, d)) for d in (1, 2, 3)]
    return finish(upper, lower)


def solution(mesh):
    fine = Mesh(
        mesh.devices.reshape(2, 4, 2, 4, 2), ("xlo", "z", "core", "y", "xhi")
    )
    pool, head = ("xlo", "z", "core"), ("y", "xhi")
    placed = (
        P(pool, None),
        P(None, head),
        P(None, head),
        P(None, head),
        P(head, None),
        P(pool + head, None, None),
        P(pool + head, None, None),
        P(),
        P(pool),
    )
    return jax.shard_map(
        body, mesh=fine, in_specs=placed, out_specs=P(pool + head, None), check_vma=False
    )
```
